256 devices in a mesh: seq: 32 (over y, z), head: 8 (over x, core).
Axes of the slice: x: 4, y: 4, z: 8, core: 2. Of those that a mesh axis runs over, the one named last changes fastest.
Arguments:
- lin_queries: bfloat16 [2, 4096, 8192], P(None, 'seq', 'head'), may hold values from -6 to 6
- lin_keys: bfloat16 [4096, 8192], P('seq', 'head'), may hold values from -6 to 6
- lin_values: bfloat16 [4096, 8192], P('seq', 'head'), may hold values from -20 to 20
- log_decay: float32 [4096, 64], P('seq', 'head'), may hold values from -1 to 0
- norm_gain: float32 [8192], P('head'), may hold values from 0.25 to 1.75
- soft_queries: bfloat16 [2, 4096, 8192], P(None, 'seq', 'head'), may hold values from -6 to 6
- soft_keys: bfloat16 [4096, 1024], P('seq', 'head'), may hold values from -6 to 6
- soft_values: bfloat16 [4096, 1024], P('seq', 'head'), may hold values from -6 to 6
- block_mask: int32 [32, 32], replicated, may hold values from 0 to 1, as said below
Outputs:
- lin_out: bfloat16 [2, 4096, 8192], P(None, 'seq', 'head')
- soft_out: bfloat16 [2, 4096, 8192], P(None, 'seq', 'head')
The draws below stay inside these ranges and needn't reach their ends.
Inputs may be any that keep to these rules, and one draw needn't show every extreme that they name: block_mask[i, i] is 1 for every block i; entries above the diagonal are not read.
All inputs are finite; a program needn't handle non-finite values.
Results may differ from the reference program's by a relative error of at most 0.02.
Values may be sent and summed in bfloat16 or wider, within the bound.
A program may use at most 128 MiB of HBM per device.

```python
import math
import jax
import jax.numpy as jnp
from jax import lax

HEAD_COUNT = 64
DH = 128
KV_HEADS = 8
TOK_DEV = 128
TILE_SPAN = 128
SEQUENCE_LENGTH = 4096
NBLK = 32


def draw_log_decay(key, part):
    key = jax.random.fold_in(key, 11)
    random_seeds = jax.random.split(key, 7)
    fast_share = 0.4
    is_fast = jax.random.uniform(random_seeds[0], (HEAD_COUNT,)) < fast_share
    fast_rate = jnp.exp(jax.random.uniform(random_seeds[1], (HEAD_COUNT,), minval=math.log(1.0 / 50.0), maxval=math.log(1.0 / 30.0)))
    slow_rate = jnp.exp(jax.random.uniform(random_seeds[2], (HEAD_COUNT,), minval=math.log(0.05), maxval=math.log(0.5))) / SEQUENCE_LENGTH
    baseline_entries = jnp.where(is_fast, fast_rate, slow_rate)
    span_factor = jnp.exp(jax.random.uniform(random_seeds[3], (SEQUENCE_LENGTH // TILE_SPAN, HEAD_COUNT), minval=math.log(0.5), maxval=math.log(2.0)))
    span_factor = jnp.repeat(span_factor, TILE_SPAN, axis=0)
    point_factor = jnp.exp(jax.random.uniform(random_seeds[4], (SEQUENCE_LENGTH, HEAD_COUNT), minval=math.log(0.6), maxval=math.log(1.6)))
    fading_exponents = -(baseline_entries[None, :] * span_factor * point_factor)
    jump_sites_list = jax.random.randint(random_seeds[5], (2, HEAD_COUNT), 0, SEQUENCE_LENGTH)
    fading_drops = jax.random.uniform(random_seeds[6], (2, HEAD_COUNT), minval=0.2, maxval=0.5)
    line_numbers = jnp.arange(SEQUENCE_LENGTH)[:, None]
    memory_jumps = jnp.where(line_numbers == jump_sites_list[0][None, :], jnp.log(1.0 - fading_drops[0])[None, :], 0.0)
    memory_jumps = memory_jumps + jnp.where(line_numbers == jump_sites_list[1][None, :], jnp.log(1.0 - fading_drops[1])[None, :], 0.0)
    return (fading_exponents + memory_jumps).astype(jnp.float32)


def draw_lin_values(key, part):
    key = jax.random.fold_in(key, 13)
    random_seeds = jax.random.split(key, 2)
    baseline_entries = jnp.clip(jax.random.normal(random_seeds[0], (SEQUENCE_LENGTH, HEAD_COUNT * DH)), -4.0, 4.0)
    ramp_top = math.log(3.0)
    head_ids = (jnp.arange(HEAD_COUNT * DH) // DH).astype(jnp.float32)
    head_ramp = ramp_top * head_ids / max(HEAD_COUNT - 1, 1)
    wobble = jax.random.uniform(random_seeds[1], (HEAD_COUNT,), minval=math.log(0.8), maxval=math.log(1.25))
    wobble = jnp.repeat(wobble, DH)
    return (baseline_entries * jnp.exp(head_ramp + wobble)[None, :]).astype(jnp.bfloat16)


def draw_soft_keys(key, part):
    base_key = jax.random.fold_in(key, 5)
    baseline_entries = jnp.clip(jax.random.normal(base_key, (SEQUENCE_LENGTH, KV_HEADS * DH)), -4.0, 4.0)
    return baseline_entries.astype(jnp.bfloat16)


def draw_soft_queries(key, part):
    base_key = jax.random.fold_in(key, 9)
    baseline_entries = jnp.clip(jax.random.normal(base_key, (2, SEQUENCE_LENGTH, HEAD_COUNT * DH)), -4.0, 4.0)
    return baseline_entries.astype(jnp.bfloat16)


def draw_block_mask(key, part):
    key = jax.random.fold_in(key, 17)
    random_bits = jax.random.randint(key, (NBLK, NBLK), 0, 2)
    diagonal = jnp.arange(NBLK)[:, None] == jnp.arange(NBLK)[None, :]
    return jnp.where(diagonal, 1, random_bits).astype(jnp.int32)


def shard_levels(own_key, shape, cuts, least, top_value):
    def one(axis_at, parts):
        steps = jax.random.uniform(jax.random.fold_in(jax.random.fold_in(own_key, 6), axis_at), (parts,), jnp.float32, least / len(cuts), top_value / len(cuts))
        return jnp.repeat(jnp.exp(steps), shape[axis_at] // parts).reshape((-1,) + (1,) * (len(shape) - axis_at - 1))

    level = one(*cuts[0])
    for cut in cuts[1:]:
        level = level * one(*cut)
    return level


def noise(own_key, extent, scale, bound, cuts=(), held_as=jnp.bfloat16):
    loudness = shard_levels(own_key, extent, cuts, -0.22, 0.18) if cuts else 1.0
    result = jax.random.normal(own_key, extent, jnp.float32) * scale * loudness
    return jnp.minimum(jnp.maximum(result, -bound), bound).astype(held_as)


def setup_inputs(seed: int = 0) -> dict:
    arg_keys = jax.random.split(jax.random.key(seed), 10)
    lin_queries = noise(arg_keys[0], (2, SEQUENCE_LENGTH, HEAD_COUNT * DH), 1.0, 6.0, ((1, 32), (2, 8)))
    lin_keys = noise(arg_keys[1], (SEQUENCE_LENGTH, HEAD_COUNT * DH), 1.0, 6.0, ((0, 32), (1, 8)))
    lin_values = draw_lin_values(jax.random.fold_in(arg_keys[9], 71), 0)
    log_decay = draw_log_decay(jax.random.fold_in(arg_keys[9], 71), 0)
    norm_gain = jnp.clip(1.0 + 0.15 * jax.random.normal(arg_keys[4], (HEAD_COUNT * DH,), jnp.float32), 0.25, 1.75)
    soft_queries = draw_soft_queries(jax.random.fold_in(arg_keys[9], 71), 0)
    soft_keys = draw_soft_keys(jax.random.fold_in(arg_keys[9], 71), 0)
    soft_values = noise(arg_keys[7], (SEQUENCE_LENGTH, KV_HEADS * DH), 1.0, 6.0, ((0, 32), (1, 8)))
    block_mask = draw_block_mask(jax.random.fold_in(arg_keys[9], 71), 0)
    return {"lin_queries": lin_queries, "lin_keys": lin_keys, "lin_values": lin_values, "log_decay": log_decay, "norm_gain": norm_gain, "soft_queries": soft_queries, "soft_keys": soft_keys, "soft_values": soft_values, "block_mask": block_mask}


def linear_pair(lin_queries, lin_keys, lin_values, log_decay):
    segment_count = SEQUENCE_LENGTH // TOK_DEV
    query_segs = lin_queries.reshape(2, segment_count, TOK_DEV, HEAD_COUNT, DH).transpose(1, 0, 2, 3, 4)
    key_segs = lin_keys.reshape(segment_count, TOK_DEV, HEAD_COUNT, DH)
    value_segs = lin_values.reshape(segment_count, TOK_DEV, HEAD_COUNT, DH)
    rate_segs = log_decay.reshape(segment_count, TOK_DEV, HEAD_COUNT)
    causal = jnp.arange(TOK_DEV)[:, None] >= jnp.arange(TOK_DEV)[None, :]

    def advance(carried, pieces):
        queries, keys_blk, values_blk, fading_exponents = pieces
        running = jnp.cumsum(fading_exponents, axis=0)
        totals = running[-1]
        keys_scaled = (keys_blk.astype(jnp.float32) * jnp.exp(totals[None, :] - running)[:, :, None]).astype(jnp.bfloat16)
        update = jnp.einsum('sha,shb->hab', keys_scaled.astype(jnp.float32), values_blk.astype(jnp.float32))
        state_b = carried.astype(jnp.bfloat16)
        from_state = jnp.exp(running)[None, :, :, None] * jnp.einsum('jtha,hab->jthb', queries.astype(jnp.float32), state_b.astype(jnp.float32))
        scores = jnp.einsum('jtha,sha->jhts', queries.astype(jnp.float32), keys_blk.astype(jnp.float32))
        decay_gap = running.T[:, :, None] - running.T[:, None, :]
        weights = jnp.where(causal[None, None], scores * jnp.exp(jnp.minimum(decay_gap, 0.0))[None], 0.0).astype(jnp.bfloat16)
        in_segment = jnp.einsum('jhts,shb->jthb', weights.astype(jnp.float32), values_blk.astype(jnp.float32))
        new_state = jnp.exp(totals)[:, None, None] * carried + update
        return (new_state, from_state + in_segment)
    start_state = jnp.zeros((HEAD_COUNT, DH, DH), jnp.float32)
    _, results = lax.scan(advance, start_state, (query_segs, key_segs, value_segs, rate_segs))
    return results.transpose(1, 0, 2, 3, 4).reshape(2, SEQUENCE_LENGTH, HEAD_COUNT * DH)

def softmax_pair(soft_in, soft_keys, soft_values, block_mask):
    positions = jnp.arange(SEQUENCE_LENGTH, dtype=jnp.int32)
    block_ids = positions // TILE_SPAN
    allowed = (block_mask[block_ids][:, block_ids] == 1) & (positions[None, :] <= positions[:, None])
    score_scale = 1.0 / math.sqrt(DH)
    group_size = HEAD_COUNT // KV_HEADS

    def one_head(head_idx):
        kv_index = head_idx // group_size
        queries = lax.dynamic_slice_in_dim(soft_in, (head_idx * DH).astype(jnp.int32), DH, 2)
        keys_head = lax.dynamic_slice_in_dim(soft_keys, (kv_index * DH).astype(jnp.int32), DH, 1)
        values_head = lax.dynamic_slice_in_dim(soft_values, (kv_index * DH).astype(jnp.int32), DH, 1)
        scores = jnp.einsum('jta,sa->jts', queries.astype(jnp.float32), keys_head.astype(jnp.float32)) * score_scale
        row_max = lax.optimization_barrier(jnp.max(jnp.where(allowed[None], scores, -1e+30), axis=-1, keepdims=True))
        probs = jnp.where(allowed[None], jnp.exp(scores - row_max), 0.0)
        row_total = lax.optimization_barrier(jnp.sum(probs, axis=-1, keepdims=True))
        blended = jnp.einsum('jts,sa->jta', probs.astype(jnp.bfloat16).astype(jnp.float32), values_head.astype(jnp.float32))
        return (blended / row_total).astype(jnp.bfloat16)
    results = lax.map(one_head, jnp.arange(HEAD_COUNT, dtype=jnp.int32))
    return results.transpose(1, 2, 0, 3).reshape(2, SEQUENCE_LENGTH, HEAD_COUNT * DH)

def reference(lin_queries, lin_keys, lin_values, log_decay, norm_gain, soft_queries, soft_keys, soft_values, block_mask):
    linear = linear_pair(lin_queries, lin_keys, lin_values, log_decay)
    mean_sq = lax.optimization_barrier(jnp.sum(linear * linear, axis=-1, keepdims=True)) / (HEAD_COUNT * DH)
    lin_out = (linear * lax.rsqrt(mean_sq + 1e-06) * norm_gain[None, None, :]).astype(jnp.bfloat16)
    soft_in = (soft_queries.astype(jnp.float32) + lin_out.astype(jnp.float32)).astype(jnp.bfloat16)
    soft_out = softmax_pair(soft_in, soft_keys, soft_values, block_mask)
    return (lin_out, soft_out)
```

```python
import math

import jax
import jax.numpy as jnp
from jax import lax
from jax.experimental import pallas as pl
from jax.experimental.pallas import tpu as pltpu
from jax.sharding import PartitionSpec as P

MESH = pl.DeviceIdType.MESH
HI = lax.Precision.HIGHEST
F32 = jnp.float32
BF16 = jnp.bfloat16

FEATURES = 8192
DH = 128
TOK = 128
HEADS = 8
NY, NZ, NX = 4, 8, 8
NSEQ = NY * NZ
NEG = -1e30
STEP_BLOCKS = 4
STEP = STEP_BLOCKS * TOK
SCALE = math.log2(math.e) / math.sqrt(DH)


def dot_t(a, b, **kw):
    return lax.dot_general(a, b, (((1,), (1,)), ((), ())), preferred_element_type=F32, **kw)


def dot_0(a, b, **kw):
    return lax.dot_general(a, b, (((0,), (0,)), ((), ())), preferred_element_type=F32, **kw)


def dot(a, b, **kw):
    return jnp.dot(a, b, preferred_element_type=F32, **kw)


def cols(h):
    return pl.ds(pl.multiple_of(h * DH, DH), DH)


def linear_kernel(
    lq_hbm, lk_hbm, lv_hbm, ld_hbm, gain_ref, sk, sv,
    lin_out, kv,
    lq, lk, lv, ld, ks, u_send, u_recv, dec_send, dec_recv, drow_send, drow_recv,
    t_send, t_recv, p_send, st, lin, sq_send, sq_recv,
    in_sem, own_sem, kv_send, kv_recv, u_ss, u_rs, d_ss, d_rs, w_ss, w_rs,
    t_ss, t_rs, p_ss, p_rs, q_ss, q_rs,
):
    me = lax.axis_index("seq")
    hd = lax.axis_index("head")
    y, z = me // NZ, me % NZ

    def zpeer(i):
        return y * NZ + (z + i + NZ) % NZ

    def ypeer(i):
        return ((y + i + NY) % NY) * NZ + z

    def to_seq(src, dst, ssem, rsem, dev):
        return pltpu.make_async_remote_copy(
            src_ref=src, dst_ref=dst, send_sem=ssem, recv_sem=rsem,
            device_id={"seq": dev}, device_id_type=MESH,
        )

    loads = [
        pltpu.make_async_copy(a, b, in_sem.at[i])
        for i, (a, b) in enumerate(((ld_hbm, ld), (lk_hbm, lk), (lv_hbm, lv), (lq_hbm, lq)))
    ]
    for c in loads:
        c.start()

    barrier = pltpu.get_barrier_semaphore()
    for i in range(1, NZ):
        pl.semaphore_signal(barrier, inc=1, device_id={"seq": zpeer(i)}, device_id_type=MESH)
    for i in range(1, NY):
        pl.semaphore_signal(barrier, inc=1, device_id={"seq": ypeer(i)}, device_id_type=MESH)
    for i in range(1, NX):
        pl.semaphore_signal(barrier, inc=1, device_id={"head": (hd + i) % NX}, device_id_type=MESH)

    loads[0].wait()
    row = lax.broadcasted_iota(jnp.int32, (TOK, TOK), 0)
    col = lax.broadcasted_iota(jnp.int32, (TOK, TOK), 1)
    tril = (row >= col).astype(F32)
    spread = (
        lax.broadcasted_iota(jnp.int32, (HEADS, DH), 0) == lax.broadcasted_iota(jnp.int32, (HEADS, DH), 1)
    ).astype(F32)
    cum = dot(tril, dot(ld[...], spread, precision=HI), precision=HI)
    cum_t = cum.T
    total = cum[TOK - 1 : TOK, :]
    dec_send[...] = jnp.broadcast_to(total, (8, DH))
    dec_recv[pl.ds(z, 1)] = jnp.broadcast_to(total, (1, 8, DH))

    pl.semaphore_wait(barrier, NZ + NY + NX - 3)

    sends = []

    def start(c):
        c.start()
        sends.append(c)

    for i in range(1, NZ):
        start(to_seq(dec_send, dec_recv.at[z], d_ss.at[i], d_rs.at[z], zpeer(i)))

    own = [pltpu.make_async_copy(a, kv.at[me, k], own_sem.at[k]) for k, a in enumerate((sk, sv))]
    for c in own:
        c.start()
    kv_count = [0]
    reach_right = (4, 3)
    reach_left = (3, 4)

    def kv_start(src, b, k, dev):
        n = kv_count[0]
        kv_count[0] += 1
        start(to_seq(src, kv.at[b, k], kv_send.at[n], kv_recv.at[b, k], dev))

    def kv_wait(b, k):
        to_seq(kv.at[b, k], kv.at[b, k], kv_send.at[0], kv_recv.at[b, k], me).wait_recv()

    def kv_own():
        for k, a in enumerate((sk, sv)):
            kv_start(a, me, k, zpeer(1))
            kv_start(a, me, k, zpeer(-1))
            kv_start(a, me, k, ypeer(1))
            kv_start(a, me, k, ypeer(-1))

    def kv_step(s):
        for k in range(2):
            if s <= reach_right[k]:
                b = zpeer(-s)
                kv_wait(b, k)
                if s < reach_right[k]:
                    kv_start(kv.at[b, k], b, k, zpeer(1))
                kv_start(kv.at[b, k], b, k, ypeer(1))
                kv_start(kv.at[b, k], b, k, ypeer(-1))
            if s <= reach_left[k]:
                b = zpeer(s)
                kv_wait(b, k)
                if s < reach_left[k]:
                    kv_start(kv.at[b, k], b, k, zpeer(-1))
                kv_start(kv.at[b, k], b, k, ypeer(1))
                kv_start(kv.at[b, k], b, k, ypeer(-1))

    def block(dy, dz):
        return ((y + dy + NY) % NY) * NZ + (z + dz + NZ) % NZ

    def kv_forward(dz):
        kv_wait(block(-1, dz), 0)
        kv_start(kv.at[block(-1, dz), 0], block(-1, dz), 0, ypeer(1))
        kv_wait(block(1, dz), 1)
        kv_start(kv.at[block(1, dz), 1], block(1, dz), 1, ypeer(-1))

    kv_own()

    loads[1].wait()
    fade = jnp.exp(total - cum)
    for h in range(HEADS):
        hs = slice(h * DH, (h + 1) * DH)
        ks[:, hs] = (lk[:, hs].astype(F32) * fade[:, h : h + 1]).astype(BF16)
    loads[2].wait()
    for i in (4, 3, 5, 2, 6, 1, 7, 0):
        h = (z + i) % NZ
        u = dot_0(ks[:, cols(h)], lv[:, cols(h)]).astype(BF16)
        if i:
            u_send[pl.ds(h, 1)] = u[None]
            start(to_seq(u_send.at[h], u_recv.at[z], u_ss.at[i], u_rs.at[z], zpeer(i)))
        else:
            u_recv[pl.ds(h, 1)] = u[None]

    kv_step(1)

    for i in range(1, NZ):
        src = (z - i + NZ) % NZ
        to_seq(dec_send, dec_recv.at[src], d_ss.at[i], d_rs.at[src], zpeer(i)).wait_recv()
    row_sum = jnp.sum(dec_recv[...], axis=0)
    drow_send[...] = row_sum
    drow_recv[pl.ds(y, 1)] = row_sum[None]
    for i in range(1, NY):
        start(to_seq(drow_send, drow_recv.at[y], w_ss.at[i], w_rs.at[y], ypeer(i)))

    loads[3].wait()
    causal = row >= col
    for h in range(HEADS):
        hs = slice(h * DH, (h + 1) * DH)
        q = lq[:, :, hs].reshape(2 * TOK, DH)
        score = dot_t(q, lk[:, hs])
        gap = jnp.exp(jnp.minimum(cum[:, h : h + 1] - cum_t[h : h + 1, :], 0.0))
        gap = jnp.where(causal, gap, 0.0)
        w = (score.reshape(2, TOK, TOK) * gap[None]).astype(BF16).reshape(2 * TOK, TOK)
        lin[h] = dot(w, lv[:, hs])
        if h == 3:
            kv_step(2)

    lane = lax.broadcasted_iota(jnp.int32, (8, DH), 1)

    def of_head(v):
        return jnp.exp(jnp.sum(jnp.where(lane == z, v, 0.0), axis=1, keepdims=True)[:1])

    decay = [of_head(dec_recv[i]) for i in range(NZ)]
    for i in range(1, NZ):
        src = (z - i + NZ) % NZ
        to_seq(u_send.at[0], u_recv.at[src], u_ss.at[i], u_rs.at[src], zpeer(i)).wait_recv()
    t = u_recv[0].astype(F32)
    for i in range(1, NZ):
        t = t * decay[i] + u_recv[i].astype(F32)
    t_send[...] = t.astype(BF16)
    t_recv[pl.ds(y, 1)] = t.astype(BF16)[None]
    for i in (2, 1, 3):
        start(to_seq(t_send, t_recv.at[y], t_ss.at[i], t_rs.at[y], ypeer(i)))

    kv_step(3)
    kv_forward(0)

    for i in range(1, NY):
        src = (y - i + NY) % NY
        to_seq(drow_send, drow_recv.at[src], w_ss.at[i], w_rs.at[src], ypeer(i)).wait_recv()
        to_seq(t_send, t_recv.at[src], t_ss.at[i], t_rs.at[src], ypeer(i)).wait_recv()
    s = jnp.zeros((DH, DH), F32)
    for i in range(NY - 1):
        s = jnp.where(i < y, s * of_head(drow_recv[i]) + t_recv[i].astype(F32), s)
    for i in range(NZ):
        p_send[i] = s.astype(BF16)
        if i < NZ - 1:
            s = s * decay[i] + u_recv[i].astype(F32)
    for i in (4, 3, 5, 2, 6, 1, 7):
        d = (z + i) % NZ
        start(to_seq(p_send.at[d], st.at[z], p_ss.at[i], p_rs.at[z], zpeer(i)))
    st[pl.ds(z, 1)] = p_send[pl.ds(z, 1)]

    kv_step(4)
    for dz in (1, -1, 2, -2):
        kv_forward(dz)

    for i in range(1, NZ):
        src = (z - i + NZ) % NZ
        to_seq(p_send.at[0], st.at[src], p_ss.at[i], p_rs.at[src], zpeer(i)).wait_recv()

    ecum = jnp.exp(cum)
    squares = jnp.zeros((2 * TOK, DH), F32)
    for h in range(HEADS):
        hs = slice(h * DH, (h + 1) * DH)
        q = lq[:, :, hs].reshape(2 * TOK, DH)
        f = dot(q, st[h]).reshape(2, TOK, DH) * ecum[:, h : h + 1][None]
        full = lin[h] + f.reshape(2 * TOK, DH)
        lin[h] = full
        squares = squares + full * full
    sq = dot_t(jnp.ones((8, DH), F32), squares, precision=HI)
    sq_send[...] = sq
    sq_recv[pl.ds(hd, 1)] = sq[None]
    for i in range(1, NX):
        start(
            pltpu.make_async_remote_copy(
                src_ref=sq_send, dst_ref=sq_recv.at[hd], send_sem=q_ss.at[i], recv_sem=q_rs.at[hd],
                device_id={"head": (hd + i) % NX}, device_id_type=MESH,
            )
        )
    for dz in (3, -3, 4):
        kv_forward(dz)
    for i in range(1, NX):
        src = (hd - i + NX) % NX
        pltpu.make_async_remote_copy(
            src_ref=sq_send, dst_ref=sq_recv.at[src], send_sem=q_ss.at[i], recv_sem=q_rs.at[src],
            device_id={"head": src}, device_id_type=MESH,
        ).wait_recv()
    mean = jnp.sum(sq_recv[...], axis=0) * (1.0 / FEATURES)
    inv = dot_0(lax.rsqrt(mean + 1e-6), jnp.full((8, DH), 0.125, F32), precision=HI)
    for h in range(HEADS):
        hs = slice(h * DH, (h + 1) * DH)
        res = lin[h] * inv * gain_ref[hs][None, :]
        lin_out[:, :, hs] = res.astype(BF16).reshape(2, TOK, DH)

    for dz in range(NZ):
        kv_wait(block(-1, dz), 1)
        kv_wait(block(1, dz), 0)
        kv_wait(block(2, dz), 0)
        kv_wait(block(2, dz), 1)
    for c in own:
        c.wait()
    for c in sends:
        c.wait_send()


def linear_part(lq, lk, lv, ld, gain, sk, sv):
    hbm = pl.BlockSpec(memory_space=pl.ANY)
    vmem = pl.BlockSpec(memory_space=pltpu.VMEM)
    dma = pltpu.SemaphoreType.DMA
    V = pltpu.VMEM
    mat = (DH, DH)
    return pl.pallas_call(
        linear_kernel,
        out_shape=(
            jax.ShapeDtypeStruct((2, TOK, HEADS * DH), BF16),
            jax.ShapeDtypeStruct((NSEQ, 2, TOK, DH), BF16),
        ),
        in_specs=[hbm, hbm, hbm, hbm, vmem, hbm, hbm],
        out_specs=(vmem, hbm),
        scratch_shapes=[
            V((2, TOK, HEADS * DH), BF16),
            V((TOK, HEADS * DH), BF16),
            V((TOK, HEADS * DH), BF16),
            V((TOK, HEADS), F32),
            V((TOK, HEADS * DH), BF16),
            V((NZ,) + mat, BF16),
            V((NZ,) + mat, BF16),
            V((8, DH), F32),
            V((NZ, 8, DH), F32),
            V((8, DH), F32),
            V((NY, 8, DH), F32),
            V(mat, BF16),
            V((NY,) + mat, BF16),
            V((NZ,) + mat, BF16),
            V((HEADS,) + mat, BF16),
            V((HEADS, 2 * TOK, DH), F32),
            V((8, 2 * TOK), F32),
            V((NX, 8, 2 * TOK), F32),
            dma((4,)),
            dma((2,)),
            dma((62,)),
            dma((NSEQ, 2)),
            dma((NZ,)), dma((NZ,)),
            dma((NZ,)), dma((NZ,)),
            dma((NY,)), dma((NY,)),
            dma((NY,)), dma((NY,)),
            dma((NZ,)), dma((NZ,)),
            dma((NX,)), dma((NX,)),
        ],
        compiler_params=pltpu.CompilerParams(
            collective_id=0, has_side_effects=True, vmem_limit_bytes=32 * 2**20
        ),
        cost_estimate=pl.CostEstimate(flops=240_000_000, bytes_accessed=5_000_000, transcendentals=300_000),
        name="linear_and_gather",
    )(lq, lk, lv, ld, gain, sk, sv)


def softmax_kernel(
    mask, lin_ref, sq_ref, kv,
    lin_out, soft_out,
    order, kaug, vaug, qaug, m_ref, acc, k_sem, v_sem,
):
    me = lax.axis_index("seq")
    order[0] = me

    def scan(b, n):
        ok = jnp.logical_and(mask[me, b] == 1, b < me)

        @pl.when(ok)
        def _():
            order[n] = b

        return n + ok.astype(jnp.int32)

    count = lax.fori_loop(0, NSEQ, scan, jnp.int32(1))
    steps = (count + STEP_BLOCKS - 1) // STEP_BLOCKS

    def pad(i, c):
        order[i] = me
        return c

    lax.fori_loop(count, steps * STEP_BLOCKS, pad, 0)

    def rows(i, size=TOK):
        return pl.ds(pl.multiple_of(i * size, size), size)

    def copies(i):
        b = order[i]
        return (
            pltpu.make_async_copy(kv.at[b, 0], kaug.at[rows(i), pl.ds(0, DH)], k_sem.at[i]),
            pltpu.make_async_copy(kv.at[b, 1], vaug.at[rows(i), pl.ds(0, DH)], v_sem.at[i]),
        )

    def load(i, c):
        for x in copies(i):
            x.start()
        return c

    lax.fori_loop(0, steps * STEP_BLOCKS, load, 0)

    row = lax.broadcasted_iota(jnp.int32, (TOK, TOK), 0)
    col = lax.broadcasted_iota(jnp.int32, (TOK, TOK), 1)

    def bias(i, c):
        kaug[rows(i), DH:] = jnp.where(i < count, 0.0, jnp.full((TOK, TOK), NEG, F32)).astype(BF16)
        vaug[rows(i), DH:] = jnp.ones((TOK, DH), BF16)
        return c

    lax.fori_loop(0, steps * STEP_BLOCKS, bias, 0)
    kaug[:TOK, DH:] = jnp.where(row <= col, 0.0, NEG).astype(BF16)
    pick = (row == col).astype(BF16)
    for h in range(HEADS):
        hs = slice(h * DH, (h + 1) * DH)
        for j in range(2):
            lin = lin_ref[j, :, hs]
            q = (sq_ref[j, :, hs].astype(F32) + lin.astype(F32)) * SCALE
            qaug[h, j * TOK : (j + 1) * TOK, :DH] = q.astype(BF16)
            qaug[h, j * TOK : (j + 1) * TOK, DH:] = pick
            lin_out[j, :, hs] = lin

    def step(i, first):
        for n in range(STEP_BLOCKS):
            for x in copies(i * STEP_BLOCKS + n):
                x.wait()
        for h in range(HEADS):
            s = dot_t(qaug[h], kaug[rows(i, STEP), :])
            top = jnp.max(s, axis=1, keepdims=True)
            if not first:
                top = jnp.maximum(m_ref[h][:, :1], top)
                keep = jnp.exp2(m_ref[h] - top)
            p = jnp.exp2(s - top).astype(BF16)
            new = dot(p, vaug[rows(i, STEP), :])
            if first:
                acc[h] = new
            else:
                acc[h, :, :DH] = acc[h, :, :DH] * keep + new[:, :DH]
                acc[h, :, DH:] = acc[h, :, DH:] * keep + new[:, DH:]
            m_ref[h] = jnp.broadcast_to(top, (2 * TOK, DH))

    step(0, True)

    def rest(i, c):
        step(i, False)
        return c

    lax.fori_loop(1, steps, rest, 0)
    for h in range(HEADS):
        hs = slice(h * DH, (h + 1) * DH)
        out = (acc[h, :, :DH] / acc[h, :, DH:]).astype(BF16)
        soft_out[:, :, hs] = out.reshape(2, TOK, DH)


def softmax_part(mask, lin, sq, kv):
    hbm = pl.BlockSpec(memory_space=pl.ANY)
    vmem = pl.BlockSpec(memory_space=pltpu.VMEM)
    V = pltpu.VMEM
    out = jax.ShapeDtypeStruct((2, TOK, HEADS * DH), BF16)
    return pl.pallas_call(
        softmax_kernel,
        out_shape=(out, out),
        in_specs=[pl.BlockSpec(memory_space=pltpu.SMEM), vmem, vmem, hbm],
        out_specs=(vmem, vmem),
        scratch_shapes=[
            pltpu.SMEM((NSEQ,), jnp.int32),
            V((NSEQ * TOK, 2 * DH), BF16),
            V((NSEQ * TOK, 2 * DH), BF16),
            V((HEADS, 2 * TOK, 2 * DH), BF16),
            V((HEADS, 2 * TOK, DH), F32),
            V((HEADS, 2 * TOK, 2 * DH), F32),
            pltpu.SemaphoreType.DMA((NSEQ,)),
            pltpu.SemaphoreType.DMA((NSEQ,)),
        ],
        compiler_params=pltpu.CompilerParams(vmem_limit_bytes=40 * 2**20),
        cost_estimate=pl.CostEstimate(flops=6_000_000_000, bytes_accessed=5_000_000, transcendentals=6_000_000),
        name="softmax_attention",
    )(mask, lin, sq, kv)


def local(lin_queries, lin_keys, lin_values, log_decay, norm_gain, soft_queries, soft_keys, soft_values, block_mask):
    lin, kv = linear_part(lin_queries, lin_keys, lin_values, log_decay, norm_gain, soft_keys, soft_values)
    return softmax_part(block_mask, lin, soft_queries, kv)


def solution(mesh):
    return jax.shard_map(
        local,
        mesh=mesh,
        in_specs=(
            P(None, "seq", "head"),
            P("seq", "head"),
            P("seq", "head"),
            P("seq", "head"),
            P("head"),
            P(None, "seq", "head"),
            P("seq", "head"),
            P("seq", "head"),
            P(),
        ),
        out_specs=(P(None, "seq", "head"), P(None, "seq", "head")),
        check_vma=False,
    )
```

```python
import math

import jax
import jax.numpy as jnp
from jax import lax
from jax.experimental import pallas as pl
from jax.experimental.pallas import tpu as pltpu
from jax.sharding import PartitionSpec as P

MESH = pl.DeviceIdType.MESH
HI = lax.Precision.HIGHEST
F32 = jnp.float32
BF16 = jnp.bfloat16

FEATURES = 8192
DH = 128
TOK = 128
HEADS = 8
NY, NZ, NX = 4, 8, 8
NSEQ = NY * NZ
NEG = -1e30
STEP_BLOCKS = 4
STEP = STEP_BLOCKS * TOK
HEAD_UNROLL = 8
U_UNROLL = 1
SCALE = math.log2(math.e) / math.sqrt(DH)


def dot_t(a, b, **kw):
    return lax.dot_general(a, b, (((1,), (1,)), ((), ())), preferred_element_type=F32, **kw)


def dot_0(a, b, **kw):
    return lax.dot_general(a, b, (((0,), (0,)), ((), ())), preferred_element_type=F32, **kw)


def dot(a, b, **kw):
    return jnp.dot(a, b, preferred_element_type=F32, **kw)


def cols(h):
    return pl.ds(pl.multiple_of(h * DH, DH), DH)


def linear_kernel(
    lq_hbm, lk_hbm, lv_hbm, ld_hbm, gain_hbm, sk, sv,
    lin_out, kv,
    lq, lk, lv, ld, gain_ref, cum_ref, colc, inv_ref, u_send, u_recv, dec_send, dec_recv, drow_send, drow_recv,
    t_send, t_recv, p_send, st, lin, sq_send, sq_recv,
    in_sem, own_sem, kv_send, kv_recv, u_ss, u_rs, d_ss, d_rs, w_ss, w_rs,
    t_ss, t_rs, p_ss, p_rs, q_ss, q_rs,
):
    me = lax.axis_index("seq")
    hd = lax.axis_index("head")
    y, z = me // NZ, me % NZ

    def zpeer(i):
        return y * NZ + (z + i + NZ) % NZ

    def ypeer(i):
        return ((y + i + NY) % NY) * NZ + z

    def to_seq(src, dst, ssem, rsem, dev):
        return pltpu.make_async_remote_copy(
            src_ref=src, dst_ref=dst, send_sem=ssem, recv_sem=rsem,
            device_id={"seq": dev}, device_id_type=MESH,
        )

    loads = [
        pltpu.make_async_copy(a, b, in_sem.at[i])
        for i, (a, b) in enumerate(((ld_hbm, ld), (lk_hbm, lk), (lv_hbm, lv), (lq_hbm, lq), (gain_hbm, gain_ref)))
    ]
    for c in loads:
        c.start()

    barrier = pltpu.get_barrier_semaphore()
    for i in range(1, NZ):
        pl.semaphore_signal(barrier, inc=1, device_id={"seq": zpeer(i)}, device_id_type=MESH)
    for i in range(1, NY):
        pl.semaphore_signal(barrier, inc=1, device_id={"seq": ypeer(i)}, device_id_type=MESH)
    for i in range(1, NX):
        pl.semaphore_signal(barrier, inc=1, device_id={"head": (hd + i) % NX}, device_id_type=MESH)

    loads[0].wait()
    row = lax.broadcasted_iota(jnp.int32, (TOK, TOK), 0)
    col = lax.broadcasted_iota(jnp.int32, (TOK, TOK), 1)
    tril = (row >= col).astype(F32)
    spread = (
        lax.broadcasted_iota(jnp.int32, (DH, HEADS), 0) == lax.broadcasted_iota(jnp.int32, (DH, HEADS), 1)
    ).astype(F32)
    cum_t = dot(spread, dot_t(ld[...], tril, precision=HI), precision=HI)
    cum_ref[...] = cum_t
    total = cum_t.T[TOK - 1 : TOK, :]
    dec_send[...] = jnp.broadcast_to(total, (8, DH))
    dec_recv[pl.ds(z, 1)] = jnp.broadcast_to(total, (1, 8, DH))

    pl.semaphore_wait(barrier, NZ + NY + NX - 3)

    sends = []

    def start(c):
        c.start()
        sends.append(c)

    for i in range(1, NZ):
        start(to_seq(dec_send, dec_recv.at[z], d_ss.at[i], d_rs.at[z], zpeer(i)))

    own = [pltpu.make_async_copy(a, kv.at[me, k], own_sem.at[k]) for k, a in enumerate((sk, sv))]
    for c in own:
        c.start()
    kv_count = [0]
    reach_right = (4, 3)
    reach_left = (3, 4)

    def kv_start(src, b, k, dev):
        n = kv_count[0]
        kv_count[0] += 1
        start(to_seq(src, kv.at[b, k], kv_send.at[n], kv_recv.at[b, k], dev))

    def kv_wait(b, k):
        to_seq(kv.at[b, k], kv.at[b, k], kv_send.at[0], kv_recv.at[b, k], me).wait_recv()

    def kv_own():
        for k, a in enumerate((sk, sv)):
            kv_start(a, me, k, zpeer(1))
            kv_start(a, me, k, zpeer(-1))
            kv_start(a, me, k, ypeer(1))
            kv_start(a, me, k, ypeer(-1))

    def kv_step(s):
        for k in range(2):
            if s <= reach_right[k]:
                b = zpeer(-s)
                kv_wait(b, k)
                if s < reach_right[k]:
                    kv_start(kv.at[b, k], b, k, zpeer(1))
                kv_start(kv.at[b, k], b, k, ypeer(1))
                kv_start(kv.at[b, k], b, k, ypeer(-1))
            if s <= reach_left[k]:
                b = zpeer(s)
                kv_wait(b, k)
                if s < reach_left[k]:
                    kv_start(kv.at[b, k], b, k, zpeer(-1))
                kv_start(kv.at[b, k], b, k, ypeer(1))
                kv_start(kv.at[b, k], b, k, ypeer(-1))

    def block(dy, dz):
        return ((y + dy + NY) % NY) * NZ + (z + dz + NZ) % NZ

    def kv_forward(dz):
        kv_wait(block(-1, dz), 0)
        kv_start(kv.at[block(-1, dz), 0], block(-1, dz), 0, ypeer(1))
        kv_wait(block(1, dz), 1)
        kv_start(kv.at[block(1, dz), 1], block(1, dz), 1, ypeer(-1))

    kv_own()

    loads[1].wait()
    loads[2].wait()

    def u_copy(i):
        h = (z + i) % NZ
        return to_seq(u_send.at[h], u_recv.at[z], u_ss.at[i], u_rs.at[z], y * NZ + h)

    def head_update(i):
        h = (z + i) % NZ
        c = jnp.broadcast_to(cum_ref[pl.ds(h, 1), :], (TOK, TOK)).T
        colc[h] = c
        k = (lk[:, cols(h)].astype(F32) * jnp.exp(c[TOK - 1 :, :] - c)).astype(BF16)
        return dot_0(k, lv[:, cols(h)]).astype(BF16)

    def update(n, c):
        i = n + 1
        u_send[pl.ds((z + i) % NZ, 1)] = head_update(i)[None]
        u_copy(i).start()
        return c

    lax.fori_loop(0, NZ - 1, update, 0, unroll=U_UNROLL)
    u_recv[pl.ds(z, 1)] = head_update(0)[None]

    kv_step(1)

    for i in range(1, NZ):
        src = (z - i + NZ) % NZ
        to_seq(dec_send, dec_recv.at[src], d_ss.at[i], d_rs.at[src], zpeer(i)).wait_recv()
    row_sum = jnp.sum(dec_recv[...], axis=0)
    drow_send[...] = row_sum
    drow_recv[pl.ds(y, 1)] = row_sum[None]
    for i in range(1, NY):
        start(to_seq(drow_send, drow_recv.at[y], w_ss.at[i], w_rs.at[y], ypeer(i)))

    loads[3].wait()
    loads[4].wait()
    causal = row >= col

    def inside(h, c):
        q = lq[:, :, cols(h)].reshape(2 * TOK, DH)
        score = dot_t(q, lk[:, cols(h)])
        gap = jnp.exp(jnp.minimum(colc[h] - cum_ref[pl.ds(h, 1), :], 0.0))
        gap = jnp.where(causal, gap, 0.0)
        w = (score.reshape(2, TOK, TOK) * gap[None]).astype(BF16).reshape(2 * TOK, TOK)
        lin[h] = dot(w, lv[:, cols(h)])
        return c

    lax.fori_loop(0, HEADS // 2, inside, 0, unroll=2)
    kv_step(2)
    lax.fori_loop(HEADS // 2, HEADS, inside, 0, unroll=2)

    lane = lax.broadcasted_iota(jnp.int32, (8, DH), 1)

    def of_head(v):
        return jnp.exp(jnp.sum(jnp.where(lane == z, v, 0.0), axis=1, keepdims=True)[:1])

    decay = [of_head(dec_recv[i]) for i in range(NZ)]
    for i in range(1, NZ):
        src = (z - i + NZ) % NZ
        to_seq(u_send.at[0], u_recv.at[src], u_ss.at[i], u_rs.at[src], zpeer(i)).wait_recv()
    t = u_recv[0].astype(F32)
    for i in range(1, NZ):
        t = t * decay[i] + u_recv[i].astype(F32)
    t_send[...] = t.astype(BF16)
    t_recv[pl.ds(y, 1)] = t.astype(BF16)[None]
    for i in (2, 1, 3):
        start(to_seq(t_send, t_recv.at[y], t_ss.at[i], t_rs.at[y], ypeer(i)))

    kv_step(3)
    kv_forward(0)

    for i in range(1, NY):
        src = (y - i + NY) % NY
        to_seq(drow_send, drow_recv.at[src], w_ss.at[i], w_rs.at[src], ypeer(i)).wait_recv()
        to_seq(t_send, t_recv.at[src], t_ss.at[i], t_rs.at[src], ypeer(i)).wait_recv()
    s = jnp.zeros((DH, DH), F32)
    for i in range(NY - 1):
        s = jnp.where(i < y, s * of_head(drow_recv[i]) + t_recv[i].astype(F32), s)
    for i in range(NZ):
        p_send[i] = s.astype(BF16)
        if i < NZ - 1:
            s = s * decay[i] + u_recv[i].astype(F32)
    for i in (4, 3, 5, 2, 6, 1, 7):
        d = (z + i) % NZ
        start(to_seq(p_send.at[d], st.at[z], p_ss.at[i], p_rs.at[z], zpeer(i)))
    st[pl.ds(z, 1)] = p_send[pl.ds(z, 1)]

    kv_step(4)
    for dz in (1, -1, 2, -2):
        kv_forward(dz)

    for i in range(1, NZ):
        src = (z - i + NZ) % NZ
        to_seq(p_send.at[0], st.at[src], p_ss.at[i], p_rs.at[src], zpeer(i)).wait_recv()

    def outer(h, squares):
        q = lq[:, :, cols(h)].reshape(2 * TOK, DH)
        f = dot(q, st[h]).reshape(2, TOK, DH) * jnp.exp(colc[h])[None]
        full = lin[h] + f.reshape(2 * TOK, DH)
        lin[h] = full
        return squares + full * full

    squares = lax.fori_loop(0, HEADS, outer, jnp.zeros((2 * TOK, DH), F32), unroll=2)
    sq = dot_t(jnp.ones((8, DH), F32), squares, precision=HI)
    sq_send[...] = sq
    sq_recv[pl.ds(hd, 1)] = sq[None]
    for i in range(1, NX):
        start(
            pltpu.make_async_remote_copy(
                src_ref=sq_send, dst_ref=sq_recv.at[hd], send_sem=q_ss.at[i], recv_sem=q_rs.at[hd],
                device_id={"head": (hd + i) % NX}, device_id_type=MESH,
            )
        )
    for dz in (3, -3, 4):
        kv_forward(dz)
    for i in range(1, NX):
        src = (hd - i + NX) % NX
        pltpu.make_async_remote_copy(
            src_ref=sq_send, dst_ref=sq_recv.at[src], send_sem=q_ss.at[i], recv_sem=q_rs.at[src],
            device_id={"head": src}, device_id_type=MESH,
        ).wait_recv()
    mean = jnp.sum(sq_recv[...], axis=0) * (1.0 / FEATURES)
    inv = dot_0(lax.rsqrt(mean + 1e-6), jnp.full((8, DH), 0.125, F32), precision=HI)
    inv_ref[...] = inv

    def scale(h, c):
        res = lin[h] * inv_ref[...] * gain_ref[cols(h)][None, :]
        lin_out[:, :, cols(h)] = res.astype(BF16).reshape(2, TOK, DH)
        return c

    lax.fori_loop(0, HEADS, scale, 0, unroll=2)

    for dz in range(NZ):
        kv_wait(block(-1, dz), 1)
        kv_wait(block(1, dz), 0)
        kv_wait(block(2, dz), 0)
        kv_wait(block(2, dz), 1)
    for c in own:
        c.wait()
    for c in sends:
        c.wait_send()
    for i in range(1, NZ):
        u_copy(i).wait_send()


def linear_part(lq, lk, lv, ld, gain, sk, sv):
    hbm = pl.BlockSpec(memory_space=pltpu.HBM)
    vmem = pl.BlockSpec(memory_space=pltpu.VMEM)
    dma = pltpu.SemaphoreType.DMA
    V = pltpu.VMEM
    mat = (DH, DH)
    return pl.pallas_call(
        linear_kernel,
        out_shape=(
            jax.ShapeDtypeStruct((2, TOK, HEADS * DH), BF16),
            jax.ShapeDtypeStruct((NSEQ, 2, TOK, DH), BF16),
        ),
        in_specs=[hbm, hbm, hbm, hbm, hbm, hbm, hbm],
        out_specs=(vmem, pl.BlockSpec(memory_space=pl.ANY)),
        scratch_shapes=[
            V((2, TOK, HEADS * DH), BF16),
            V((TOK, HEADS * DH), BF16),
            V((TOK, HEADS * DH), BF16),
            V((HEADS, TOK), F32),
            V((HEADS * DH,), F32),
            V(mat, F32),
            V((HEADS,) + mat, F32),
            V((2 * TOK, DH), F32),
            V((NZ,) + mat, BF16),
            V((NZ,) + mat, BF16),
            V((8, DH), F32),
            V((NZ, 8, DH), F32),
            V((8, DH), F32),
            V((NY, 8, DH), F32),
            V(mat, BF16),
            V((NY,) + mat, BF16),
            V((NZ,) + mat, BF16),
            V((HEADS,) + mat, BF16),
            V((HEADS, 2 * TOK, DH), F32),
            V((8, 2 * TOK), F32),
            V((NX, 8, 2 * TOK), F32),
            dma((5,)),
            dma((2,)),
            dma((62,)),
            dma((NSEQ, 2)),
            dma((NZ,)), dma((NZ,)),
            dma((NZ,)), dma((NZ,)),
            dma((NY,)), dma((NY,)),
            dma((NY,)), dma((NY,)),
            dma((NZ,)), dma((NZ,)),
            dma((NX,)), dma((NX,)),
        ],
        compiler_params=pltpu.CompilerParams(
            collective_id=0, has_side_effects=True, vmem_limit_bytes=56 * 2**20
        ),
        cost_estimate=pl.CostEstimate(flops=240_000_000, bytes_accessed=5_000_000, transcendentals=300_000),
        name="linear_and_gather",
    )(lq, lk, lv, ld, gain, sk, sv)


def softmax_kernel(
    mask_hbm, lin_hbm, sq_hbm, kv,
    lin_out, soft_out,
    mask, lin_ref, sq_ref, res, order, kaug, vaug, qaug, m_ref, acc, in_sem, out_sem, k_sem, v_sem,
):
    me = lax.axis_index("seq")

    def rows(i, size=TOK):
        return pl.ds(pl.multiple_of(i * size, size), size)

    def copies(i, b):
        return (
            pltpu.make_async_copy(kv.at[b, 0], kaug.at[rows(i), pl.ds(0, DH)], k_sem.at[i]),
            pltpu.make_async_copy(kv.at[b, 1], vaug.at[rows(i), pl.ds(0, DH)], v_sem.at[i]),
        )

    loads = [
        pltpu.make_async_copy(a, b, in_sem.at[i])
        for i, (a, b) in enumerate(((mask_hbm, mask), (lin_hbm, lin_ref), (sq_hbm, sq_ref)))
    ]
    for c in loads:
        c.start()
    for c in copies(0, me):
        c.start()

    row = lax.broadcasted_iota(jnp.int32, (TOK, TOK), 0)
    col = lax.broadcasted_iota(jnp.int32, (TOK, TOK), 1)
    pick = (row == col).astype(BF16)
    kaug[:TOK, DH:] = jnp.where(row <= col, 0.0, NEG).astype(BF16)
    vaug[:, DH:] = jnp.ones((NSEQ * TOK, DH), BF16)

    loads[0].wait()
    order[0] = me
    count = jnp.int32(1)
    for b in range(NSEQ - 1):
        order[count] = b
        count = count + jnp.where(b < me, mask[me, b], 0)
    steps = (count + STEP_BLOCKS - 1) // STEP_BLOCKS
    for n in range(STEP_BLOCKS - 1):
        order[count + n] = me

    def load(i, c):
        for x in copies(i, order[i]):
            x.start()
        kaug[rows(i), DH:] = jnp.broadcast_to(jnp.where(i < count, 0.0, NEG), (TOK, TOK)).astype(BF16)
        return c

    lax.fori_loop(1, steps * STEP_BLOCKS, load, 0)
    m_ref[...] = jnp.full_like(m_ref, -3e38)
    acc[...] = jnp.zeros_like(acc)
    loads[1].wait()
    keep_lin = pltpu.make_async_copy(lin_ref, lin_out, out_sem.at[HEADS])
    keep_lin.start()
    loads[2].wait()

    def prepare(h, c):
        for j in range(2):
            q = (sq_ref[j, :, cols(h)].astype(F32) + lin_ref[j, :, cols(h)].astype(F32)) * SCALE
            qaug[h, j * TOK : (j + 1) * TOK, :DH] = q.astype(BF16)
            qaug[h, j * TOK : (j + 1) * TOK, DH:] = pick
        return c

    lax.fori_loop(0, HEADS, prepare, 0, unroll=2)

    def step(i, c):
        for n in range(STEP_BLOCKS):
            for x in copies(i * STEP_BLOCKS + n, me):
                x.wait()

        def head(h, c):
            s = dot_t(qaug[h], kaug[rows(i, STEP), :])
            old = m_ref[h]
            top = jnp.maximum(old, jnp.max(s, axis=1, keepdims=True))
            m_ref[h] = top
            keep = jnp.exp2(old - top)
            p = jnp.concatenate(
                [jnp.exp2(s[:, n * DH : (n + 1) * DH] - top).astype(BF16) for n in range(STEP_BLOCKS)], axis=1
            )
            new = dot(p, vaug[rows(i, STEP), :])
            acc[h, :, :DH] = acc[h, :, :DH] * keep + new[:, :DH]
            acc[h, :, DH:] = acc[h, :, DH:] * keep + new[:, DH:]
            return c

        return lax.fori_loop(0, HEADS, head, c, unroll=HEAD_UNROLL)

    lax.fori_loop(0, steps, step, 0)

    def out_copy(h):
        return pltpu.make_async_copy(res.at[h], soft_out.at[:, :, cols(h)], out_sem.at[h])

    def finish(h, c):
        res[h] = (acc[h, :, :DH] / acc[h, :, DH:]).astype(BF16).reshape(2, TOK, DH)
        out_copy(h).start()
        return c

    lax.fori_loop(0, HEADS, finish, 0, unroll=2)
    keep_lin.wait()
    for h in range(HEADS):
        out_copy(h).wait()


def softmax_part(mask, lin, sq, kv):
    hbm = pl.BlockSpec(memory_space=pl.ANY)
    V = pltpu.VMEM
    out = jax.ShapeDtypeStruct((2, TOK, HEADS * DH), BF16)
    return pl.pallas_call(
        softmax_kernel,
        out_shape=(out, out),
        in_specs=[hbm] * 4,
        out_specs=(hbm, hbm),
        scratch_shapes=[
            pltpu.SMEM((NSEQ, NSEQ), jnp.int32),
            V((2, TOK, HEADS * DH), BF16),
            V((2, TOK, HEADS * DH), BF16),
            V((HEADS, 2, TOK, DH), BF16),
            pltpu.SMEM((NSEQ + STEP_BLOCKS,), jnp.int32),
            V((NSEQ * TOK, 2 * DH), BF16),
            V((NSEQ * TOK, 2 * DH), BF16),
            V((HEADS, 2 * TOK, 2 * DH), BF16),
            V((HEADS, 2 * TOK, DH), F32),
            V((HEADS, 2 * TOK, 2 * DH), F32),
            pltpu.SemaphoreType.DMA((3,)),
            pltpu.SemaphoreType.DMA((HEADS + 1,)),
            pltpu.SemaphoreType.DMA((NSEQ,)),
            pltpu.SemaphoreType.DMA((NSEQ,)),
        ],
        compiler_params=pltpu.CompilerParams(vmem_limit_bytes=56 * 2**20),
        cost_estimate=pl.CostEstimate(flops=6_000_000_000, bytes_accessed=5_000_000, transcendentals=6_000_000),
        name="softmax_attention",
    )(mask, lin, sq, kv)


def local(lin_queries, lin_keys, lin_values, log_decay, norm_gain, soft_queries, soft_keys, soft_values, block_mask):
    lin, kv = linear_part(lin_queries, lin_keys, lin_values, log_decay.T, norm_gain, soft_keys, soft_values)
    return softmax_part(block_mask, lin, soft_queries, kv)


def solution(mesh):
    return jax.shard_map(
        local,
        mesh=mesh,
        in_specs=(
            P(None, "seq", "head"),
            P("seq", "head"),
            P("seq", "head"),
            P("seq", "head"),
            P("head"),
            P(None, "seq", "head"),
            P("seq", "head"),
            P("seq", "head"),
            P(),
        ),
        out_specs=(P(None, "seq", "head"), P(None, "seq", "head")),
        check_vma=False,
    )
```

```python
import math

import jax
import jax.numpy as jnp
from jax import lax
from jax.experimental import pallas as pl
from jax.experimental.pallas import tpu as pltpu
from jax.sharding import PartitionSpec as P

MESH = pl.DeviceIdType.MESH
HI = lax.Precision.HIGHEST
F32 = jnp.float32
BF16 = jnp.bfloat16

FEATURES = 8192
DH = 128
TOK = 128
HEADS = 8
NY, NZ, NX = 4, 8, 8
NSEQ = NY * NZ
NEG = -1e30
STEP_BLOCKS = 8
STEP = STEP_BLOCKS * TOK
HEAD_UNROLL = 8
U_UNROLL = 1
SCALE = math.log2(math.e) / math.sqrt(DH)


def dot_t(a, b, **kw):
    return lax.dot_general(a, b, (((1,), (1,)), ((), ())), preferred_element_type=F32, **kw)


def dot_0(a, b, **kw):
    return lax.dot_general(a, b, (((0,), (0,)), ((), ())), preferred_element_type=F32, **kw)


def dot(a, b, **kw):
    return jnp.dot(a, b, preferred_element_type=F32, **kw)


def cols(h):
    return pl.ds(pl.multiple_of(h * DH, DH), DH)


def linear_kernel(
    lq_hbm, lk_hbm, lv_hbm, ld_hbm, gain_hbm, sk, sv, sq_hbm,
    lin_out, q_out, k_all, v_all,
    lq, lk, lv, ld, gain_ref, sq_in, lin_res, q_res, cum_ref, colc, inv_ref, u_send, u_recv, dec_send, dec_recv, drow_send, drow_recv,
    t_send, t_recv, p_send, st, lin, sq_send, sq_recv,
    in_sem, out_sem, own_sem, kv_send, kv_recv, u_ss, u_rs, d_ss, d_rs, w_ss, w_rs,
    t_ss, t_rs, p_ss, p_rs, q_ss, q_rs,
):
    me = lax.axis_index("seq")
    hd = lax.axis_index("head")
    y, z = me // NZ, me % NZ

    def zpeer(i):
        return y * NZ + (z + i + NZ) % NZ

    def ypeer(i):
        return ((y + i + NY) % NY) * NZ + z

    def to_seq(src, dst, ssem, rsem, dev):
        return pltpu.make_async_remote_copy(
            src_ref=src, dst_ref=dst, send_sem=ssem, recv_sem=rsem,
            device_id={"seq": dev}, device_id_type=MESH,
        )

    loads = [
        pltpu.make_async_copy(a, b, in_sem.at[i])
        for i, (a, b) in enumerate(((ld_hbm, ld), (lk_hbm, lk), (lv_hbm, lv), (lq_hbm, lq), (gain_hbm, gain_ref), (sq_hbm, sq_in)))
    ]
    for c in loads:
        c.start()

    barrier = pltpu.get_barrier_semaphore()
    for i in range(1, NZ):
        pl.semaphore_signal(barrier, inc=1, device_id={"seq": zpeer(i)}, device_id_type=MESH)
    for i in range(1, NY):
        pl.semaphore_signal(barrier, inc=1, device_id={"seq": ypeer(i)}, device_id_type=MESH)
    for i in range(1, NX):
        pl.semaphore_signal(barrier, inc=1, device_id={"head": (hd + i) % NX}, device_id_type=MESH)

    loads[0].wait()
    row = lax.broadcasted_iota(jnp.int32, (TOK, TOK), 0)
    col = lax.broadcasted_iota(jnp.int32, (TOK, TOK), 1)
    tril = (row >= col).astype(F32)
    cum_t = dot_t(ld[...], tril, precision=HI)
    cum_ref[...] = cum_t
    total = jnp.broadcast_to(cum_t[:, TOK - 1 :], (HEADS, DH))
    dec_send[...] = total
    dec_recv[pl.ds(z, 1)] = total[None]

    pl.semaphore_wait(barrier, NZ + NY + NX - 3)

    sends = []

    def start(c):
        c.start()
        sends.append(c)

    for i in range(1, NZ):
        start(to_seq(dec_send, dec_recv.at[z], d_ss.at[i], d_rs.at[z], zpeer(i)))

    def slot(b, k):
        return (k_all, v_all)[k].at[pl.ds(pl.multiple_of(b * TOK, TOK), TOK)]

    own = [pltpu.make_async_copy(a, slot(me, k), own_sem.at[k]) for k, a in enumerate((sk, sv))]
    for c in own:
        c.start()
    kv_count = [0]
    reach_right = (4, 3)
    reach_left = (3, 4)

    def kv_start(src, b, k, dev):
        n = kv_count[0]
        kv_count[0] += 1
        start(to_seq(src, slot(b, k), kv_send.at[n], kv_recv.at[b, k], dev))

    def kv_wait(b, k):
        to_seq(slot(b, k), slot(b, k), kv_send.at[0], kv_recv.at[b, k], me).wait_recv()

    def kv_own():
        for k, a in enumerate((sk, sv)):
            kv_start(a, me, k, zpeer(1))
            kv_start(a, me, k, zpeer(-1))
            kv_start(a, me, k, ypeer(1))
            kv_start(a, me, k, ypeer(-1))

    def kv_step(s):
        for k in range(2):
            if s <= reach_right[k]:
                b = zpeer(-s)
                kv_wait(b, k)
                if s < reach_right[k]:
                    kv_start(slot(b, k), b, k, zpeer(1))
                kv_start(slot(b, k), b, k, ypeer(1))
                kv_start(slot(b, k), b, k, ypeer(-1))
            if s <= reach_left[k]:
                b = zpeer(s)
                kv_wait(b, k)
                if s < reach_left[k]:
                    kv_start(slot(b, k), b, k, zpeer(-1))
                kv_start(slot(b, k), b, k, ypeer(1))
                kv_start(slot(b, k), b, k, ypeer(-1))

    def block(dy, dz):
        return ((y + dy + NY) % NY) * NZ + (z + dz + NZ) % NZ

    def kv_forward(dz):
        kv_wait(block(-1, dz), 0)
        kv_start(slot(block(-1, dz), 0), block(-1, dz), 0, ypeer(1))
        kv_wait(block(1, dz), 1)
        kv_start(slot(block(1, dz), 1), block(1, dz), 1, ypeer(-1))

    kv_own()

    loads[1].wait()
    loads[2].wait()

    def u_copy(i):
        h = (z + i) % NZ
        return to_seq(u_send.at[h], u_recv.at[z], u_ss.at[i], u_rs.at[z], y * NZ + h)

    def head_update(i):
        h = (z + i) % NZ
        c = jnp.broadcast_to(cum_ref[pl.ds(h, 1), :], (TOK, TOK)).T
        colc[h] = c
        k = (lk[:, cols(h)].astype(F32) * jnp.exp(c[TOK - 1 :, :] - c)).astype(BF16)
        return dot_0(k, lv[:, cols(h)]).astype(BF16)

    def update(n, c):
        i = n + 1
        u_send[pl.ds((z + i) % NZ, 1)] = head_update(i)[None]
        u_copy(i).start()
        return c

    lax.fori_loop(0, NZ - 1, update, 0, unroll=U_UNROLL)
    u_recv[pl.ds(z, 1)] = head_update(0)[None]

    kv_step(1)

    for i in range(1, NZ):
        src = (z - i + NZ) % NZ
        to_seq(dec_send, dec_recv.at[src], d_ss.at[i], d_rs.at[src], zpeer(i)).wait_recv()
    row_sum = jnp.sum(dec_recv[...], axis=0)
    drow_send[...] = row_sum
    drow_recv[pl.ds(y, 1)] = row_sum[None]
    for i in range(1, NY):
        start(to_seq(drow_send, drow_recv.at[y], w_ss.at[i], w_rs.at[y], ypeer(i)))

    loads[3].wait()
    loads[4].wait()
    loads[5].wait()
    causal = row >= col

    def inside(h, c):
        q = lq[:, :, cols(h)].reshape(2 * TOK, DH)
        score = dot_t(q, lk[:, cols(h)])
        gap = jnp.exp(jnp.minimum(colc[h] - cum_ref[pl.ds(h, 1), :], 0.0))
        gap = jnp.where(causal, gap, 0.0)
        w = (score.reshape(2, TOK, TOK) * gap[None]).astype(BF16).reshape(2 * TOK, TOK)
        lin[h] = dot(w, lv[:, cols(h)])
        return c

    lax.fori_loop(0, HEADS // 2, inside, 0, unroll=2)
    kv_step(2)
    lax.fori_loop(HEADS // 2, HEADS, inside, 0, unroll=2)

    def of_head(ref, i):
        return jnp.exp(ref[i, pl.ds(z, 1), :])

    decay = [of_head(dec_recv, i) for i in range(NZ)]
    for i in range(1, NZ):
        src = (z - i + NZ) % NZ
        to_seq(u_send.at[0], u_recv.at[src], u_ss.at[i], u_rs.at[src], zpeer(i)).wait_recv()
    t = u_recv[0].astype(F32)
    for i in range(1, NZ):
        t = t * decay[i] + u_recv[i].astype(F32)
    t_send[...] = t.astype(BF16)
    t_recv[pl.ds(y, 1)] = t.astype(BF16)[None]
    for i in (2, 1, 3):
        start(to_seq(t_send, t_recv.at[y], t_ss.at[i], t_rs.at[y], ypeer(i)))

    kv_step(3)
    kv_forward(0)

    for i in range(1, NY):
        src = (y - i + NY) % NY
        to_seq(drow_send, drow_recv.at[src], w_ss.at[i], w_rs.at[src], ypeer(i)).wait_recv()
        to_seq(t_send, t_recv.at[src], t_ss.at[i], t_rs.at[src], ypeer(i)).wait_recv()
    s = jnp.zeros((DH, DH), F32)
    for i in range(NY - 1):
        s = jnp.where(i < y, s * of_head(drow_recv, i) + t_recv[i].astype(F32), s)
    for i in range(NZ):
        p_send[i] = s.astype(BF16)
        if i < NZ - 1:
            s = s * decay[i] + u_recv[i].astype(F32)
    for i in (4, 3, 5, 2, 6, 1, 7):
        d = (z + i) % NZ
        start(to_seq(p_send.at[d], st.at[z], p_ss.at[i], p_rs.at[z], zpeer(i)))
    st[pl.ds(z, 1)] = p_send[pl.ds(z, 1)]

    kv_step(4)
    for dz in (1, -1, 2, -2, 3, -3, 4):
        kv_forward(dz)

    squares = jnp.zeros((2 * TOK, DH), F32)
    for i in (0, 4, 3, 5, 2, 6, 1, 7):
        h = (z - i + NZ) % NZ
        if i:
            to_seq(p_send.at[0], st.at[h], p_ss.at[i], p_rs.at[h], zpeer(i)).wait_recv()
        q = lq[:, :, cols(h)].reshape(2 * TOK, DH)
        f = dot(q, st[h]).reshape(2, TOK, DH) * jnp.exp(colc[h])[None]
        full = lin[h] + f.reshape(2 * TOK, DH)
        lin[h] = full
        squares = squares + full * full
    sq = dot_t(jnp.ones((8, DH), F32), squares, precision=HI)
    sq_send[...] = sq
    sq_recv[pl.ds(hd, 1)] = sq[None]
    for i in range(1, NX):
        start(
            pltpu.make_async_remote_copy(
                src_ref=sq_send, dst_ref=sq_recv.at[hd], send_sem=q_ss.at[i], recv_sem=q_rs.at[hd],
                device_id={"head": (hd + i) % NX}, device_id_type=MESH,
            )
        )
    for i in range(1, NX):
        src = (hd - i + NX) % NX
        pltpu.make_async_remote_copy(
            src_ref=sq_send, dst_ref=sq_recv.at[src], send_sem=q_ss.at[i], recv_sem=q_rs.at[src],
            device_id={"head": src}, device_id_type=MESH,
        ).wait_recv()
    mean = jnp.sum(sq_recv[...], axis=0) * (1.0 / FEATURES)
    inv = dot_0(lax.rsqrt(mean + 1e-6), jnp.full((8, DH), 0.125, F32), precision=HI)
    inv_ref[...] = inv

    def result_copies(h):
        return (
            pltpu.make_async_copy(lin_res.at[h], lin_out.at[:, :, cols(h)], out_sem.at[0, h]),
            pltpu.make_async_copy(q_res.at[h], q_out.at[:, :, cols(h)], out_sem.at[1, h]),
        )

    def scale(h, c):
        res = (lin[h] * inv_ref[...] * gain_ref[cols(h)][None, :]).astype(BF16).reshape(2, TOK, DH)
        lin_res[h] = res
        q_res[h] = ((sq_in[:, :, cols(h)].astype(F32) + res.astype(F32)) * SCALE).astype(BF16)
        for x in result_copies(h):
            x.start()
        return c

    lax.fori_loop(0, HEADS, scale, 0, unroll=2)

    for dz in range(NZ):
        kv_wait(block(-1, dz), 1)
        kv_wait(block(1, dz), 0)
        kv_wait(block(2, dz), 0)
        kv_wait(block(2, dz), 1)
    for h in range(HEADS):
        for x in result_copies(h):
            x.wait()
    for c in own:
        c.wait()
    for c in sends:
        c.wait_send()
    for i in range(1, NZ):
        u_copy(i).wait_send()


def linear_part(*operands):
    hbm = pl.BlockSpec(memory_space=pl.ANY)
    dma = pltpu.SemaphoreType.DMA
    V = pltpu.VMEM
    mat = (DH, DH)
    return pl.pallas_call(
        linear_kernel,
        out_shape=(
            jax.ShapeDtypeStruct((2, TOK, HEADS * DH), BF16),
            jax.ShapeDtypeStruct((2, TOK, HEADS * DH), BF16),
            jax.ShapeDtypeStruct((NSEQ * TOK, DH), BF16),
            jax.ShapeDtypeStruct((NSEQ * TOK, DH), BF16),
        ),
        in_specs=[hbm] * 8,
        out_specs=(hbm,) * 4,
        scratch_shapes=[
            V((2, TOK, HEADS * DH), BF16),
            V((TOK, HEADS * DH), BF16),
            V((TOK, HEADS * DH), BF16),
            V((HEADS, TOK), F32),
            V((HEADS * DH,), F32),
            V((2, TOK, HEADS * DH), BF16),
            V((HEADS, 2, TOK, DH), BF16),
            V((HEADS, 2, TOK, DH), BF16),
            V((HEADS, DH), F32),
            V((HEADS,) + mat, F32),
            V((2 * TOK, DH), F32),
            V((NZ,) + mat, BF16),
            V((NZ,) + mat, BF16),
            V((8, DH), F32),
            V((NZ, 8, DH), F32),
            V((8, DH), F32),
            V((NY, 8, DH), F32),
            V(mat, BF16),
            V((NY,) + mat, BF16),
            V((NZ,) + mat, BF16),
            V((HEADS,) + mat, BF16),
            V((HEADS, 2 * TOK, DH), F32),
            V((8, 2 * TOK), F32),
            V((NX, 8, 2 * TOK), F32),
            dma((6,)),
            dma((2, HEADS)),
            dma((2,)),
            dma((62,)),
            dma((NSEQ, 2)),
            dma((NZ,)), dma((NZ,)),
            dma((NZ,)), dma((NZ,)),
            dma((NY,)), dma((NY,)),
            dma((NY,)), dma((NY,)),
            dma((NZ,)), dma((NZ,)),
            dma((NX,)), dma((NX,)),
        ],
        compiler_params=pltpu.CompilerParams(
            collective_id=0, has_side_effects=True, vmem_limit_bytes=56 * 2**20
        ),
        cost_estimate=pl.CostEstimate(flops=240_000_000, bytes_accessed=5_000_000, transcendentals=300_000),
        name="linear_and_gather",
    )(*operands)


def softmax_kernel(
    mask_hbm, lin_hbm, q_hbm, k_all, v_all,
    lin_out, soft_out,
    mask, lin_ref, res, order, kaug, vaug, qaug, m_ref, acc, in_sem, out_sem, q_sem, k_sem, v_sem,
):
    me = lax.axis_index("seq")

    def rows(i, size=TOK):
        return pl.ds(pl.multiple_of(i * size, size), size)

    def copies(i):
        r = rows(i, STEP)
        return (
            pltpu.make_async_copy(k_all.at[r], kaug.at[r, pl.ds(0, DH)], k_sem.at[i]),
            pltpu.make_async_copy(v_all.at[r], vaug.at[r, pl.ds(0, DH)], v_sem.at[i]),
        )

    fetch_mask = pltpu.make_async_copy(mask_hbm, mask, in_sem.at[0])
    fetch_mask.start()
    parts = me // STEP_BLOCKS + 1

    def load(i, c):
        for x in copies(i):
            x.start()
        return c

    lax.fori_loop(0, parts, load, 0)
    fetch_q = [
        pltpu.make_async_copy(
            q_hbm.at[j, :, pl.ds(h * DH, DH)], qaug.at[h, pl.ds(j * TOK, TOK), pl.ds(0, DH)], q_sem.at[h, j]
        )
        for h in range(HEADS)
        for j in range(2)
    ]
    for c in fetch_q:
        c.start()
    fetch_lin = pltpu.make_async_copy(lin_hbm, lin_ref, in_sem.at[1])
    fetch_lin.start()

    row = lax.broadcasted_iota(jnp.int32, (TOK, TOK), 0)
    col = lax.broadcasted_iota(jnp.int32, (TOK, TOK), 1)
    pick = (row == col).astype(BF16)
    for h in range(HEADS):
        for j in range(2):
            qaug[h, j * TOK : (j + 1) * TOK, DH:] = pick
    kaug[:, DH:] = jnp.zeros(((NSEQ + 1) * TOK, DH), BF16)
    vaug[:, DH:] = jnp.ones(((NSEQ + 1) * TOK, DH), BF16)
    kaug[NSEQ * TOK :, :DH] = jnp.zeros((TOK, DH), BF16)
    vaug[NSEQ * TOK :, :DH] = jnp.zeros((TOK, DH), BF16)
    kaug[NSEQ * TOK :, DH:] = jnp.full((TOK, DH), NEG, F32).astype(BF16)
    kaug[rows(me), DH:] = jnp.where(row <= col, 0.0, NEG).astype(BF16)
    m_ref[...] = jnp.full_like(m_ref, -3e38)
    acc[...] = jnp.zeros_like(acc)

    fetch_mask.wait()
    order[0] = me
    count = jnp.int32(1)
    for b in range(NSEQ - 1):
        order[count] = b
        count = count + jnp.where(b < me, mask[me, b], 0)
    steps = (count + STEP_BLOCKS - 1) // STEP_BLOCKS
    for n in range(STEP_BLOCKS - 1):
        order[count + n] = NSEQ

    for c in fetch_q:
        c.wait()
    fetch_lin.wait()
    keep_lin = pltpu.make_async_copy(lin_ref, lin_out, out_sem.at[HEADS])
    keep_lin.start()

    def arrive(i, c):
        for x in copies(i):
            x.wait()
        return c

    lax.fori_loop(0, parts, arrive, 0)

    def step(i, c):
        places = [rows(order[i * STEP_BLOCKS + n]) for n in range(STEP_BLOCKS)]

        def head(h, c):
            s = dot_t(qaug[h], jnp.concatenate([kaug[r, :] for r in places], axis=0))
            old = m_ref[h]
            top = jnp.maximum(old, jnp.max(s, axis=1, keepdims=True))
            m_ref[h] = top
            keep = jnp.exp2(old - top)
            p = jnp.concatenate(
                [jnp.exp2(s[:, n * DH : (n + 1) * DH] - top).astype(BF16) for n in range(STEP_BLOCKS)], axis=1
            )
            new = dot(p, jnp.concatenate([vaug[r, :] for r in places], axis=0))
            acc[h, :, :DH] = acc[h, :, :DH] * keep + new[:, :DH]
            acc[h, :, DH:] = acc[h, :, DH:] * keep + new[:, DH:]
            return c

        return lax.fori_loop(0, HEADS, head, c, unroll=HEAD_UNROLL)

    lax.fori_loop(0, steps, step, 0)

    def out_copy(h):
        return pltpu.make_async_copy(res.at[h], soft_out.at[:, :, cols(h)], out_sem.at[h])

    def finish(h, c):
        res[h] = (acc[h, :, :DH] / acc[h, :, DH:]).astype(BF16).reshape(2, TOK, DH)
        out_copy(h).start()
        return c

    lax.fori_loop(0, HEADS, finish, 0, unroll=2)
    keep_lin.wait()
    for h in range(HEADS):
        out_copy(h).wait()


def softmax_part(*operands):
    hbm = pl.BlockSpec(memory_space=pl.ANY)
    V = pltpu.VMEM
    out = jax.ShapeDtypeStruct((2, TOK, HEADS * DH), BF16)
    return pl.pallas_call(
        softmax_kernel,
        out_shape=(out, out),
        in_specs=[hbm] * 5,
        out_specs=(hbm, hbm),
        scratch_shapes=[
            pltpu.SMEM((NSEQ, NSEQ), jnp.int32),
            V((2, TOK, HEADS * DH), BF16),
            V((HEADS, 2, TOK, DH), BF16),
            pltpu.SMEM((NSEQ + STEP_BLOCKS,), jnp.int32),
            V(((NSEQ + 1) * TOK, 2 * DH), BF16),
            V(((NSEQ + 1) * TOK, 2 * DH), BF16),
            V((HEADS, 2 * TOK, 2 * DH), BF16),
            V((HEADS, 2 * TOK, DH), F32),
            V((HEADS, 2 * TOK, 2 * DH), F32),
            pltpu.SemaphoreType.DMA((2,)),
            pltpu.SemaphoreType.DMA((HEADS + 1,)),
            pltpu.SemaphoreType.DMA((HEADS, 2)),
            pltpu.SemaphoreType.DMA((NSEQ // STEP_BLOCKS,)),
            pltpu.SemaphoreType.DMA((NSEQ // STEP_BLOCKS,)),
        ],
        compiler_params=pltpu.CompilerParams(vmem_limit_bytes=56 * 2**20),
        cost_estimate=pl.CostEstimate(flops=6_000_000_000, bytes_accessed=5_000_000, transcendentals=6_000_000),
        name="softmax_attention",
    )(*operands)


def local(lin_queries, lin_keys, lin_values, log_decay, norm_gain, soft_queries, soft_keys, soft_values, block_mask):
    lin, q, k_all, v_all = linear_part(
        lin_queries, lin_keys, lin_values, log_decay.T, norm_gain, soft_keys, soft_values, soft_queries
    )
    return softmax_part(block_mask, lin, q, k_all, v_all)


def solution(mesh):
    return jax.shard_map(
        local,
        mesh=mesh,
        in_specs=(
            P(None, "seq", "head"),
            P("seq", "head"),
            P("seq", "head"),
            P("seq", "head"),
            P("head"),
            P(None, "seq", "head"),
            P("seq", "head"),
            P("seq", "head"),
            P(),
        ),
        out_specs=(P(None, "seq", "head"), P(None, "seq", "head")),
        check_vma=False,
    )
```

```python
import math

import jax
import jax.numpy as jnp
from jax import lax
from jax.experimental import pallas as pl
from jax.experimental.pallas import tpu as pltpu
from jax.sharding import PartitionSpec as P

MESH = pl.DeviceIdType.MESH
HI = lax.Precision.HIGHEST
F32 = jnp.float32
BF16 = jnp.bfloat16

FEATURES = 8192
DH = 128
TOK = 128
HEADS = 8
NY, NZ, NX = 4, 8, 8
NSEQ = NY * NZ
NEG = -1e30
STEP_BLOCKS = 8
STEP = STEP_BLOCKS * TOK
HEAD_UNROLL = 8
U_UNROLL = 1
SCALE = math.log2(math.e) / math.sqrt(DH)


def dot_t(a, b, **kw):
    return lax.dot_general(a, b, (((1,), (1,)), ((), ())), preferred_element_type=F32, **kw)


def dot_0(a, b, **kw):
    return lax.dot_general(a, b, (((0,), (0,)), ((), ())), preferred_element_type=F32, **kw)


def dot(a, b, **kw):
    return jnp.dot(a, b, preferred_element_type=F32, **kw)


def cols(h):
    return pl.ds(pl.multiple_of(h * DH, DH), DH)


def linear_kernel(
    lq_hbm, lk_hbm, lv_hbm, ld_hbm, gain_hbm, sk, sv, sq_hbm,
    lin_out, q_out, k_all, v_all,
    lq, lk, lv, ld, gain_ref, sq_in, lin_res, q_res, state_ref, cum_ref, colc, inv_ref, u_send, u_recv, dec_send, dec_recv, drow_send, drow_recv,
    t_send, t_recv, p_send, st, lin, sq_send, sq_recv,
    in_sem, out_sem, own_sem, kv_send, kv_recv, u_ss, u_rs, d_ss, d_rs, w_ss, w_rs,
    t_ss, t_rs, p_ss, p_rs, q_ss, q_rs,
):
    me = lax.axis_index("seq")
    hd = lax.axis_index("head")
    y, z = me // NZ, me % NZ

    def zpeer(i):
        return y * NZ + (z + i + NZ) % NZ

    def ypeer(i):
        return ((y + i + NY) % NY) * NZ + z

    def to_seq(src, dst, ssem, rsem, dev):
        return pltpu.make_async_remote_copy(
            src_ref=src, dst_ref=dst, send_sem=ssem, recv_sem=rsem,
            device_id={"seq": dev}, device_id_type=MESH,
        )

    loads = [
        pltpu.make_async_copy(a, b, in_sem.at[i])
        for i, (a, b) in enumerate(((ld_hbm, ld), (lk_hbm, lk), (lv_hbm, lv), (lq_hbm, lq), (gain_hbm, gain_ref), (sq_hbm, sq_in)))
    ]
    for c in loads:
        c.start()

    barrier = pltpu.get_barrier_semaphore()
    for i in range(1, NZ):
        pl.semaphore_signal(barrier, inc=1, device_id={"seq": zpeer(i)}, device_id_type=MESH)
    for i in range(1, NY):
        pl.semaphore_signal(barrier, inc=1, device_id={"seq": ypeer(i)}, device_id_type=MESH)
    for i in range(1, NX):
        pl.semaphore_signal(barrier, inc=1, device_id={"head": (hd + i) % NX}, device_id_type=MESH)

    loads[0].wait()
    row = lax.broadcasted_iota(jnp.int32, (TOK, TOK), 0)
    col = lax.broadcasted_iota(jnp.int32, (TOK, TOK), 1)
    tril = (row >= col).astype(F32)
    cum_t = dot_t(ld[...], tril, precision=HI)
    cum_ref[...] = cum_t
    total = jnp.broadcast_to(cum_t[:, TOK - 1 :], (HEADS, DH))
    dec_send[...] = total
    dec_recv[pl.ds(z, 1)] = total[None]

    pl.semaphore_wait(barrier, NZ + NY + NX - 3)

    sends = []

    def start(c):
        c.start()
        sends.append(c)

    for i in range(1, NZ):
        start(to_seq(dec_send, dec_recv.at[z], d_ss.at[i], d_rs.at[z], zpeer(i)))

    def slot(b, k):
        return (k_all, v_all)[k].at[pl.ds(pl.multiple_of(b * TOK, TOK), TOK)]

    own = [pltpu.make_async_copy(a, slot(me, k), own_sem.at[k]) for k, a in enumerate((sk, sv))]
    for c in own:
        c.start()
    kv_count = [0]
    reach_right = (4, 3)
    reach_left = (3, 4)

    def kv_start(src, b, k, dev):
        n = kv_count[0]
        kv_count[0] += 1
        start(to_seq(src, slot(b, k), kv_send.at[n], kv_recv.at[b, k], dev))

    def kv_wait(b, k):
        to_seq(slot(b, k), slot(b, k), kv_send.at[0], kv_recv.at[b, k], me).wait_recv()

    def kv_own():
        for k, a in enumerate((sk, sv)):
            kv_start(a, me, k, zpeer(1))
            kv_start(a, me, k, zpeer(-1))
            kv_start(a, me, k, ypeer(1))
            kv_start(a, me, k, ypeer(-1))

    def kv_step(s):
        for k in range(2):
            if s <= reach_right[k]:
                b = zpeer(-s)
                kv_wait(b, k)
                if s < reach_right[k]:
                    kv_start(slot(b, k), b, k, zpeer(1))
                kv_start(slot(b, k), b, k, ypeer(1))
                kv_start(slot(b, k), b, k, ypeer(-1))
            if s <= reach_left[k]:
                b = zpeer(s)
                kv_wait(b, k)
                if s < reach_left[k]:
                    kv_start(slot(b, k), b, k, zpeer(-1))
                kv_start(slot(b, k), b, k, ypeer(1))
                kv_start(slot(b, k), b, k, ypeer(-1))

    def block(dy, dz):
        return ((y + dy + NY) % NY) * NZ + (z + dz + NZ) % NZ

    def kv_forward(dz):
        kv_wait(block(-1, dz), 0)
        kv_start(slot(block(-1, dz), 0), block(-1, dz), 0, ypeer(1))
        kv_wait(block(1, dz), 1)
        kv_start(slot(block(1, dz), 1), block(1, dz), 1, ypeer(-1))

    kv_own()

    loads[1].wait()
    loads[2].wait()

    def u_copy(i):
        h = (z + i) % NZ
        return to_seq(u_send.at[h], u_recv.at[z], u_ss.at[i], u_rs.at[z], y * NZ + h)

    def head_update(i):
        h = (z + i) % NZ
        c = jnp.broadcast_to(cum_ref[pl.ds(h, 1), :], (TOK, TOK)).T
        colc[h] = c
        k = (lk[:, cols(h)].astype(F32) * jnp.exp(c[TOK - 1 :, :] - c)).astype(BF16)
        return dot_0(k, lv[:, cols(h)]).astype(BF16)

    def update(n, c):
        i = n + 1
        u_send[pl.ds((z + i) % NZ, 1)] = head_update(i)[None]
        u_copy(i).start()
        return c

    lax.fori_loop(0, NZ - 1, update, 0, unroll=U_UNROLL)
    u_recv[pl.ds(z, 1)] = head_update(0)[None]

    kv_step(1)

    for i in range(1, NZ):
        src = (z - i + NZ) % NZ
        to_seq(dec_send, dec_recv.at[src], d_ss.at[i], d_rs.at[src], zpeer(i)).wait_recv()
    row_sum = jnp.sum(dec_recv[...], axis=0)
    drow_send[...] = row_sum
    drow_recv[pl.ds(y, 1)] = row_sum[None]
    for i in range(1, NY):
        start(to_seq(drow_send, drow_recv.at[y], w_ss.at[i], w_rs.at[y], ypeer(i)))

    loads[3].wait()
    loads[4].wait()
    loads[5].wait()
    causal = row >= col

    def inside(h, c):
        q = lq[:, :, cols(h)].reshape(2 * TOK, DH)
        score = dot_t(q, lk[:, cols(h)])
        gap = jnp.exp(jnp.minimum(colc[h] - cum_ref[pl.ds(h, 1), :], 0.0))
        gap = jnp.where(causal, gap, 0.0)
        w = (score.reshape(2, TOK, TOK) * gap[None]).astype(BF16).reshape(2 * TOK, TOK)
        lin[h] = dot(w, lv[:, cols(h)])
        return c

    lax.fori_loop(0, HEADS // 2, inside, 0, unroll=2)
    kv_step(2)
    lax.fori_loop(HEADS // 2, HEADS, inside, 0, unroll=2)

    def of_head(ref, i):
        return jnp.exp(ref[i, pl.ds(z, 1), :])

    decay = [of_head(dec_recv, i) for i in range(NZ)]
    for i in range(1, NZ):
        src = (z - i + NZ) % NZ
        to_seq(u_send.at[0], u_recv.at[src], u_ss.at[i], u_rs.at[src], zpeer(i)).wait_recv()
    t = u_recv[0].astype(F32)
    for i in range(1, NZ):
        t = t * decay[i] + u_recv[i].astype(F32)
    t_send[...] = t.astype(BF16)
    t_recv[pl.ds(y, 1)] = t.astype(BF16)[None]
    def total_copy(i, row_of):
        return to_seq(t_send, t_recv.at[row_of], t_ss.at[i], t_rs.at[row_of], ypeer(i))

    for i in (3, 2, 1):

        @pl.when(y + i < NY)
        def _(i=i):
            total_copy(i, y).start()


    kv_step(3)
    kv_forward(0)

    for i in range(1, NY):
        src = (y - i + NY) % NY
        to_seq(drow_send, drow_recv.at[src], w_ss.at[i], w_rs.at[src], ypeer(i)).wait_recv()

        @pl.when(y >= i)
        def _(i=i, src=src):
            total_copy(i, src).wait_recv()

    state_ref[...] = jnp.zeros((DH, DH), F32)
    for i in range(NY - 1):

        @pl.when(i < y)
        def _(i=i):
            state_ref[...] = state_ref[...] * of_head(drow_recv, i) + t_recv[i].astype(F32)

    s = state_ref[...]
    for i in range(NZ):
        p_send[i] = s.astype(BF16)
        if i < NZ - 1:
            s = s * decay[i] + u_recv[i].astype(F32)
    for i in (4, 3, 5, 2, 6, 1, 7):
        d = (z + i) % NZ
        start(to_seq(p_send.at[d], st.at[z], p_ss.at[i], p_rs.at[z], zpeer(i)))
    st[pl.ds(z, 1)] = p_send[pl.ds(z, 1)]

    kv_step(4)
    for dz in (1, -1, 2, -2):
        kv_forward(dz)

    squares = jnp.zeros((2 * TOK, DH), F32)
    for i in (0, 4, 3, 5, 2, 6, 1, 7):
        h = (z - i + NZ) % NZ
        if i:
            to_seq(p_send.at[0], st.at[h], p_ss.at[i], p_rs.at[h], zpeer(i)).wait_recv()
        q = lq[:, :, cols(h)].reshape(2 * TOK, DH)
        f = dot(q, st[h]).reshape(2, TOK, DH) * jnp.exp(colc[h])[None]
        full = lin[h] + f.reshape(2 * TOK, DH)
        lin[h] = full
        squares = squares + full * full
        if i in (3, 2, 1):
            kv_forward({3: 3, 2: -3, 1: 4}[i])
    sq = dot_t(jnp.ones((8, DH), F32), squares, precision=HI)
    sq_send[...] = sq
    sq_recv[pl.ds(hd, 1)] = sq[None]
    for i in range(1, NX):
        start(
            pltpu.make_async_remote_copy(
                src_ref=sq_send, dst_ref=sq_recv.at[hd], send_sem=q_ss.at[i], recv_sem=q_rs.at[hd],
                device_id={"head": (hd + i) % NX}, device_id_type=MESH,
            )
        )
    for i in range(1, NX):
        src = (hd - i + NX) % NX
        pltpu.make_async_remote_copy(
            src_ref=sq_send, dst_ref=sq_recv.at[src], send_sem=q_ss.at[i], recv_sem=q_rs.at[src],
            device_id={"head": src}, device_id_type=MESH,
        ).wait_recv()
    mean = jnp.sum(sq_recv[...], axis=0) * (1.0 / FEATURES)
    inv = dot_0(lax.rsqrt(mean + 1e-6), jnp.full((8, DH), 0.125, F32), precision=HI)
    inv_ref[...] = inv

    def result_copies(h):
        return (
            pltpu.make_async_copy(lin_res.at[h], lin_out.at[:, :, cols(h)], out_sem.at[0, h]),
            pltpu.make_async_copy(q_res.at[h], q_out.at[:, :, cols(h)], out_sem.at[1, h]),
        )

    def scale(h, c):
        res = (lin[h] * inv_ref[...] * gain_ref[cols(h)][None, :]).astype(BF16).reshape(2, TOK, DH)
        lin_res[h] = res
        q_res[h] = ((sq_in[:, :, cols(h)].astype(F32) + res.astype(F32)) * SCALE).astype(BF16)
        for x in result_copies(h):
            x.start()
        return c

    lax.fori_loop(0, HEADS, scale, 0, unroll=2)

    for dz in range(NZ):
        kv_wait(block(-1, dz), 1)
        kv_wait(block(1, dz), 0)
        kv_wait(block(2, dz), 0)
        kv_wait(block(2, dz), 1)
    for h in range(HEADS):
        for x in result_copies(h):
            x.wait()
    for c in own:
        c.wait()
    for c in sends:
        c.wait_send()
    for i in range(1, NZ):
        u_copy(i).wait_send()
    for i in range(1, NY):

        @pl.when(y + i < NY)
        def _(i=i):
            total_copy(i, y).wait_send()


def linear_part(*operands):
    hbm = pl.BlockSpec(memory_space=pl.ANY)
    dma = pltpu.SemaphoreType.DMA
    V = pltpu.VMEM
    mat = (DH, DH)
    return pl.pallas_call(
        linear_kernel,
        out_shape=(
            jax.ShapeDtypeStruct((2, TOK, HEADS * DH), BF16),
            jax.ShapeDtypeStruct((2, TOK, HEADS * DH), BF16),
            jax.ShapeDtypeStruct((NSEQ * TOK, DH), BF16),
            jax.ShapeDtypeStruct((NSEQ * TOK, DH), BF16),
        ),
        in_specs=[hbm] * 8,
        out_specs=(hbm,) * 4,
        scratch_shapes=[
            V((2, TOK, HEADS * DH), BF16),
            V((TOK, HEADS * DH), BF16),
            V((TOK, HEADS * DH), BF16),
            V((HEADS, TOK), F32),
            V((HEADS * DH,), F32),
            V((2, TOK, HEADS * DH), BF16),
            V((HEADS, 2, TOK, DH), BF16),
            V((HEADS, 2, TOK, DH), BF16),
            V(mat, F32),
            V((HEADS, DH), F32),
            V((HEADS,) + mat, F32),
            V((2 * TOK, DH), F32),
            V((NZ,) + mat, BF16),
            V((NZ,) + mat, BF16),
            V((8, DH), F32),
            V((NZ, 8, DH), F32),
            V((8, DH), F32),
            V((NY, 8, DH), F32),
            V(mat, BF16),
            V((NY,) + mat, BF16),
            V((NZ,) + mat, BF16),
            V((HEADS,) + mat, BF16),
            V((HEADS, 2 * TOK, DH), F32),
            V((8, 2 * TOK), F32),
            V((NX, 8, 2 * TOK), F32),
            dma((6,)),
            dma((2, HEADS)),
            dma((2,)),
            dma((62,)),
            dma((NSEQ, 2)),
            dma((NZ,)), dma((NZ,)),
            dma((NZ,)), dma((NZ,)),
            dma((NY,)), dma((NY,)),
            dma((NY,)), dma((NY,)),
            dma((NZ,)), dma((NZ,)),
            dma((NX,)), dma((NX,)),
        ],
        compiler_params=pltpu.CompilerParams(
            collective_id=0, has_side_effects=True, vmem_limit_bytes=56 * 2**20
        ),
        cost_estimate=pl.CostEstimate(flops=240_000_000, bytes_accessed=5_000_000, transcendentals=300_000),
        name="linear_and_gather",
    )(*operands)


def softmax_kernel(
    mask_hbm, lin_hbm, q_hbm, k_all, v_all,
    lin_out, soft_out,
    mask, lin_ref, res, order, kaug, vaug, qaug, m_ref, acc, in_sem, out_sem, q_sem, k_sem, v_sem,
):
    me = lax.axis_index("seq")

    def rows(i, size=TOK):
        return pl.ds(pl.multiple_of(i * size, size), size)

    def copies(i):
        r = rows(i, STEP)
        return (
            pltpu.make_async_copy(k_all.at[r], kaug.at[r, pl.ds(0, DH)], k_sem.at[i]),
            pltpu.make_async_copy(v_all.at[r], vaug.at[r, pl.ds(0, DH)], v_sem.at[i]),
        )

    fetch_mask = pltpu.make_async_copy(mask_hbm, mask, in_sem.at[0])
    fetch_mask.start()
    parts = me // STEP_BLOCKS + 1

    def load(i, c):
        for x in copies(i):
            x.start()
        return c

    lax.fori_loop(0, parts, load, 0)
    fetch_q = [
        pltpu.make_async_copy(
            q_hbm.at[j, :, pl.ds(h * DH, DH)], qaug.at[h, pl.ds(j * TOK, TOK), pl.ds(0, DH)], q_sem.at[h, j]
        )
        for h in range(HEADS)
        for j in range(2)
    ]
    for c in fetch_q:
        c.start()
    fetch_lin = pltpu.make_async_copy(lin_hbm, lin_ref, in_sem.at[1])
    fetch_lin.start()

    row = lax.broadcasted_iota(jnp.int32, (TOK, TOK), 0)
    col = lax.broadcasted_iota(jnp.int32, (TOK, TOK), 1)
    pick = (row == col).astype(BF16)
    for h in range(HEADS):
        for j in range(2):
            qaug[h, j * TOK : (j + 1) * TOK, DH:] = pick
    kaug[:, DH:] = jnp.zeros(((NSEQ + 1) * TOK, DH), BF16)
    vaug[:, DH:] = jnp.ones(((NSEQ + 1) * TOK, DH), BF16)
    kaug[NSEQ * TOK :, :DH] = jnp.zeros((TOK, DH), BF16)
    vaug[NSEQ * TOK :, :DH] = jnp.zeros((TOK, DH), BF16)
    kaug[NSEQ * TOK :, DH:] = jnp.full((TOK, DH), NEG, F32).astype(BF16)
    kaug[rows(me), DH:] = jnp.where(row <= col, 0.0, NEG).astype(BF16)
    m_ref[...] = jnp.full_like(m_ref, -3e38)
    acc[...] = jnp.zeros_like(acc)

    fetch_mask.wait()
    order[0] = me
    count = jnp.int32(1)
    for b in range(NSEQ - 1):
        order[count] = b
        count = count + jnp.where(b < me, mask[me, b], 0)
    steps = (count + STEP_BLOCKS - 1) // STEP_BLOCKS
    for n in range(STEP_BLOCKS - 1):
        order[count + n] = NSEQ

    for c in fetch_q:
        c.wait()
    fetch_lin.wait()
    keep_lin = pltpu.make_async_copy(lin_ref, lin_out, out_sem.at[HEADS])
    keep_lin.start()

    def arrive(i, c):
        for x in copies(i):
            x.wait()
        return c

    lax.fori_loop(0, parts, arrive, 0)

    def step(i, c):
        places = [rows(order[i * STEP_BLOCKS + n]) for n in range(STEP_BLOCKS)]

        def head(h, c):
            s = dot_t(qaug[h], jnp.concatenate([kaug[r, :] for r in places], axis=0))
            old = m_ref[h]
            top = jnp.maximum(old, jnp.max(s, axis=1, keepdims=True))
            m_ref[h] = top
            keep = jnp.exp2(old - top)
            p = jnp.concatenate(
                [jnp.exp2(s[:, n * DH : (n + 1) * DH] - top).astype(BF16) for n in range(STEP_BLOCKS)], axis=1
            )
            new = dot(p, jnp.concatenate([vaug[r, :] for r in places], axis=0))
            acc[h, :, :DH] = acc[h, :, :DH] * keep + new[:, :DH]
            acc[h, :, DH:] = acc[h, :, DH:] * keep + new[:, DH:]
            return c

        return lax.fori_loop(0, HEADS, head, c, unroll=HEAD_UNROLL)

    lax.fori_loop(0, steps, step, 0)

    def out_copy(h):
        return pltpu.make_async_copy(res.at[h], soft_out.at[:, :, cols(h)], out_sem.at[h])

    def finish(h, c):
        res[h] = (acc[h, :, :DH] / acc[h, :, DH:]).astype(BF16).reshape(2, TOK, DH)
        out_copy(h).start()
        return c

    lax.fori_loop(0, HEADS, finish, 0, unroll=2)
    keep_lin.wait()
    for h in range(HEADS):
        out_copy(h).wait()


def softmax_part(*operands):
    hbm = pl.BlockSpec(memory_space=pl.ANY)
    V = pltpu.VMEM
    out = jax.ShapeDtypeStruct((2, TOK, HEADS * DH), BF16)
    return pl.pallas_call(
        softmax_kernel,
        out_shape=(out, out),
        in_specs=[hbm] * 5,
        out_specs=(hbm, hbm),
        scratch_shapes=[
            pltpu.SMEM((NSEQ, NSEQ), jnp.int32),
            V((2, TOK, HEADS * DH), BF16),
            V((HEADS, 2, TOK, DH), BF16),
            pltpu.SMEM((NSEQ + STEP_BLOCKS,), jnp.int32),
            V(((NSEQ + 1) * TOK, 2 * DH), BF16),
            V(((NSEQ + 1) * TOK, 2 * DH), BF16),
            V((HEADS, 2 * TOK, 2 * DH), BF16),
            V((HEADS, 2 * TOK, DH), F32),
            V((HEADS, 2 * TOK, 2 * DH), F32),
            pltpu.SemaphoreType.DMA((2,)),
            pltpu.SemaphoreType.DMA((HEADS + 1,)),
            pltpu.SemaphoreType.DMA((HEADS, 2)),
            pltpu.SemaphoreType.DMA((NSEQ // STEP_BLOCKS,)),
            pltpu.SemaphoreType.DMA((NSEQ // STEP_BLOCKS,)),
        ],
        compiler_params=pltpu.CompilerParams(vmem_limit_bytes=56 * 2**20),
        cost_estimate=pl.CostEstimate(flops=6_000_000_000, bytes_accessed=5_000_000, transcendentals=6_000_000),
        name="softmax_attention",
    )(*operands)


def local(lin_queries, lin_keys, lin_values, log_decay, norm_gain, soft_queries, soft_keys, soft_values, block_mask):
    lin, q, k_all, v_all = linear_part(
        lin_queries, lin_keys, lin_values, log_decay.T, norm_gain, soft_keys, soft_values, soft_queries
    )
    return softmax_part(block_mask, lin, q, k_all, v_all)


def solution(mesh):
    return jax.shard_map(
        local,
        mesh=mesh,
        in_specs=(
            P(None, "seq", "head"),
            P("seq", "head"),
            P("seq", "head"),
            P("seq", "head"),
            P("head"),
            P(None, "seq", "head"),
            P("seq", "head"),
            P("seq", "head"),
            P(),
        ),
        out_specs=(P(None, "seq", "head"), P(None, "seq", "head")),
        check_vma=False,
    )
```

```python
import math

import jax
import jax.numpy as jnp
from jax import lax
from jax.experimental import pallas as pl
from jax.experimental.pallas import tpu as pltpu
from jax.sharding import PartitionSpec as P

MESH = pl.DeviceIdType.MESH
HI = lax.Precision.HIGHEST
F32 = jnp.float32
BF16 = jnp.bfloat16

FEATURES = 8192
DH = 128
TOK = 128
HEADS = 8
NY, NZ, NX = 4, 8, 8
NSEQ = NY * NZ
NEG = -1e30
STEP_BLOCKS = 8
STEP = STEP_BLOCKS * TOK
HEAD_UNROLL = 8
U_UNROLL = 1
SCALE = math.log2(math.e) / math.sqrt(DH)


def dot_t(a, b, **kw):
    return lax.dot_general(a, b, (((1,), (1,)), ((), ())), preferred_element_type=F32, **kw)


def dot_0(a, b, **kw):
    return lax.dot_general(a, b, (((0,), (0,)), ((), ())), preferred_element_type=F32, **kw)


def dot(a, b, **kw):
    return jnp.dot(a, b, preferred_element_type=F32, **kw)


def cols(h):
    return pl.ds(pl.multiple_of(h * DH, DH), DH)


def linear_kernel(
    lq_hbm, lk_hbm, lv_hbm, ld_hbm, gain_hbm, sk, sv, sq_hbm,
    lin_out, q_out, k_all, v_all,
    lq, lk, lv, ld, gain_ref, sq_in, lin_res, q_res, state_ref, cum_ref, colc, inv_ref, u_send, u_recv, dec_send, dec_recv, drow_send, drow_recv,
    t_send, t_recv, p_send, st, lin, sq_send, sq_recv,
    in_sem, out_sem, own_sem, kv_send, kv_recv, u_ss, u_rs, d_ss, d_rs, w_ss, w_rs,
    t_ss, t_rs, p_ss, p_rs, q_ss, q_rs,
):
    me = lax.axis_index("seq")
    hd = lax.axis_index("head")
    y, z = me // NZ, me % NZ

    def zpeer(i):
        return y * NZ + (z + i + NZ) % NZ

    def ypeer(i):
        return ((y + i + NY) % NY) * NZ + z

    def to_seq(src, dst, ssem, rsem, dev):
        return pltpu.make_async_remote_copy(
            src_ref=src, dst_ref=dst, send_sem=ssem, recv_sem=rsem,
            device_id={"seq": dev}, device_id_type=MESH,
        )

    loads = [
        pltpu.make_async_copy(a, b, in_sem.at[i])
        for i, (a, b) in enumerate(((ld_hbm, ld), (lk_hbm, lk), (lv_hbm, lv), (lq_hbm, lq), (gain_hbm, gain_ref), (sq_hbm, sq_in)))
    ]
    for c in loads:
        c.start()

    barrier = pltpu.get_barrier_semaphore()
    for i in range(1, NZ):
        pl.semaphore_signal(barrier, inc=1, device_id={"seq": zpeer(i)}, device_id_type=MESH)
    for i in range(1, NY):
        pl.semaphore_signal(barrier, inc=1, device_id={"seq": ypeer(i)}, device_id_type=MESH)
    for i in range(1, NX):
        pl.semaphore_signal(barrier, inc=1, device_id={"head": (hd + i) % NX}, device_id_type=MESH)

    loads[0].wait()
    row = lax.broadcasted_iota(jnp.int32, (TOK, TOK), 0)
    col = lax.broadcasted_iota(jnp.int32, (TOK, TOK), 1)
    tril = (row >= col).astype(F32)
    cum_t = dot_t(ld[...], tril, precision=HI)
    cum_ref[...] = cum_t
    total = jnp.broadcast_to(cum_t[:, TOK - 1 :], (HEADS, DH))
    dec_send[...] = total
    dec_recv[pl.ds(z, 1)] = total[None]

    pl.semaphore_wait(barrier, NZ + NY + NX - 3)

    sends = []

    def start(c):
        c.start()
        sends.append(c)

    for i in range(1, NZ):
        start(to_seq(dec_send, dec_recv.at[z], d_ss.at[i], d_rs.at[z], zpeer(i)))

    def slot(b, k):
        return (k_all, v_all)[k].at[pl.ds(pl.multiple_of(b * TOK, TOK), TOK)]

    own = [pltpu.make_async_copy(a, slot(me, k), own_sem.at[k]) for k, a in enumerate((sk, sv))]
    for c in own:
        c.start()
    kv_count = [0]
    reach_right = (4, 3)
    reach_left = (3, 4)

    def kv_start(src, b, k, dev):
        n = kv_count[0]
        kv_count[0] += 1
        start(to_seq(src, slot(b, k), kv_send.at[n], kv_recv.at[b, k], dev))

    def kv_wait(b, k):
        to_seq(slot(b, k), slot(b, k), kv_send.at[0], kv_recv.at[b, k], me).wait_recv()

    def kv_own():
        for k, a in enumerate((sk, sv)):
            kv_start(a, me, k, zpeer(1))
            kv_start(a, me, k, zpeer(-1))
            kv_start(a, me, k, ypeer(1))
            kv_start(a, me, k, ypeer(-1))

    def kv_step(s):
        for k in range(2):
            if s <= reach_right[k]:
                b = zpeer(-s)
                kv_wait(b, k)
                if s < reach_right[k]:
                    kv_start(slot(b, k), b, k, zpeer(1))
                kv_start(slot(b, k), b, k, ypeer(1))
                kv_start(slot(b, k), b, k, ypeer(-1))
            if s <= reach_left[k]:
                b = zpeer(s)
                kv_wait(b, k)
                if s < reach_left[k]:
                    kv_start(slot(b, k), b, k, zpeer(-1))
                kv_start(slot(b, k), b, k, ypeer(1))
                kv_start(slot(b, k), b, k, ypeer(-1))

    def block(dy, dz):
        return ((y + dy + NY) % NY) * NZ + (z + dz + NZ) % NZ

    def kv_forward(dz):
        kv_wait(block(-1, dz), 0)
        kv_start(slot(block(-1, dz), 0), block(-1, dz), 0, ypeer(1))
        kv_wait(block(1, dz), 1)
        kv_start(slot(block(1, dz), 1), block(1, dz), 1, ypeer(-1))

    kv_own()

    loads[1].wait()
    loads[2].wait()

    def u_copy(i):
        h = (z + i) % NZ
        return to_seq(u_send.at[h], u_recv.at[z], u_ss.at[i], u_rs.at[z], y * NZ + h)

    def head_update(i):
        h = (z + i) % NZ
        c = jnp.broadcast_to(cum_ref[pl.ds(h, 1), :], (TOK, TOK)).T
        colc[h] = c
        k = (lk[:, cols(h)].astype(F32) * jnp.exp(c[TOK - 1 :, :] - c)).astype(BF16)
        return dot_0(k, lv[:, cols(h)]).astype(BF16)

    def update(n, c):
        i = n + 1
        u_send[pl.ds((z + i) % NZ, 1)] = head_update(i)[None]
        u_copy(i).start()
        return c

    lax.fori_loop(0, NZ - 1, update, 0, unroll=U_UNROLL)
    u_recv[pl.ds(z, 1)] = head_update(0)[None]

    kv_step(1)

    for i in range(1, NZ):
        src = (z - i + NZ) % NZ
        to_seq(dec_send, dec_recv.at[src], d_ss.at[i], d_rs.at[src], zpeer(i)).wait_recv()
    row_sum = jnp.sum(dec_recv[...], axis=0)
    drow_send[...] = row_sum
    drow_recv[pl.ds(y, 1)] = row_sum[None]
    for i in range(1, NY):
        start(to_seq(drow_send, drow_recv.at[y], w_ss.at[i], w_rs.at[y], ypeer(i)))

    loads[3].wait()
    loads[4].wait()
    loads[5].wait()
    causal = row >= col

    def inside(h, c):
        q = lq[:, :, cols(h)].reshape(2 * TOK, DH)
        score = dot_t(q, lk[:, cols(h)])
        gap = jnp.exp(jnp.minimum(colc[h] - cum_ref[pl.ds(h, 1), :], 0.0))
        gap = jnp.where(causal, gap, 0.0)
        w = (score.reshape(2, TOK, TOK) * gap[None]).astype(BF16).reshape(2 * TOK, TOK)
        lin[h] = dot(w, lv[:, cols(h)])
        return c

    lax.fori_loop(0, HEADS // 2, inside, 0, unroll=2)
    kv_step(2)
    lax.fori_loop(HEADS // 2, HEADS, inside, 0, unroll=2)

    def of_head(ref, i):
        return jnp.exp(ref[i, pl.ds(z, 1), :])

    decay = [of_head(dec_recv, i) for i in range(NZ)]
    for i in range(1, NZ):
        src = (z - i + NZ) % NZ
        to_seq(u_send.at[0], u_recv.at[src], u_ss.at[i], u_rs.at[src], zpeer(i)).wait_recv()
    t = u_recv[0].astype(F32)
    for i in range(1, NZ):
        t = t * decay[i] + u_recv[i].astype(F32)
    t_send[...] = t.astype(BF16)
    t_recv[pl.ds(y, 1)] = t.astype(BF16)[None]
    def total_copy(i, row_of):
        return to_seq(t_send, t_recv.at[row_of], t_ss.at[i], t_rs.at[row_of], ypeer(i))

    for i in (3, 2, 1):

        @pl.when(y + i < NY)
        def _(i=i):
            total_copy(i, y).start()


    kv_step(3)
    kv_forward(0)

    for i in range(1, NY):
        src = (y - i + NY) % NY
        to_seq(drow_send, drow_recv.at[src], w_ss.at[i], w_rs.at[src], ypeer(i)).wait_recv()

        @pl.when(y >= i)
        def _(i=i, src=src):
            total_copy(i, src).wait_recv()

    state_ref[...] = jnp.zeros((DH, DH), F32)
    for i in range(NY - 1):

        @pl.when(i < y)
        def _(i=i):
            state_ref[...] = state_ref[...] * of_head(drow_recv, i) + t_recv[i].astype(F32)

    s = state_ref[...]
    for i in range(NZ):
        p_send[i] = s.astype(BF16)
        if i < NZ - 1:
            s = s * decay[i] + u_recv[i].astype(F32)
    for i in (4, 3, 5, 2, 6, 1, 7):
        d = (z + i) % NZ
        start(to_seq(p_send.at[d], st.at[z], p_ss.at[i], p_rs.at[z], zpeer(i)))
    st[pl.ds(z, 1)] = p_send[pl.ds(z, 1)]

    kv_step(4)
    for dz in (1, -1, 2, -2):
        kv_forward(dz)

    squares = jnp.zeros((2 * TOK, DH), F32)
    for i in (0, 4, 3, 5, 2, 6, 1, 7):
        h = (z - i + NZ) % NZ
        if i:
            to_seq(p_send.at[0], st.at[h], p_ss.at[i], p_rs.at[h], zpeer(i)).wait_recv()
        q = lq[:, :, cols(h)].reshape(2 * TOK, DH)
        f = dot(q, st[h]).reshape(2, TOK, DH) * jnp.exp(colc[h])[None]
        full = lin[h] + f.reshape(2 * TOK, DH)
        lin[h] = full
        squares = squares + full * full
        if i in (3, 2, 1):
            kv_forward({3: 3, 2: -3, 1: 4}[i])
    for j in range(2):
        part = jnp.sum(squares[j * TOK : (j + 1) * TOK, :].T, axis=0, keepdims=True)
        sq_send[:, j * TOK : (j + 1) * TOK] = jnp.broadcast_to(part, (8, TOK))
    sq_recv[pl.ds(hd, 1)] = sq_send[...][None]
    for i in range(1, NX):
        start(
            pltpu.make_async_remote_copy(
                src_ref=sq_send, dst_ref=sq_recv.at[hd], send_sem=q_ss.at[i], recv_sem=q_rs.at[hd],
                device_id={"head": (hd + i) % NX}, device_id_type=MESH,
            )
        )
    for i in range(1, NX):
        src = (hd - i + NX) % NX
        pltpu.make_async_remote_copy(
            src_ref=sq_send, dst_ref=sq_recv.at[src], send_sem=q_ss.at[i], recv_sem=q_rs.at[src],
            device_id={"head": src}, device_id_type=MESH,
        ).wait_recv()
    mean = jnp.sum(sq_recv[...], axis=0) * (1.0 / FEATURES)
    inv = lax.rsqrt(mean + 1e-6)
    for j in range(2):
        part = inv[:1, j * TOK : (j + 1) * TOK]
        inv_ref[j * TOK : (j + 1) * TOK, :] = jnp.broadcast_to(part, (TOK, TOK)).T

    def result_copies(h):
        return (
            pltpu.make_async_copy(lin_res.at[h], lin_out.at[:, :, cols(h)], out_sem.at[0, h]),
            pltpu.make_async_copy(q_res.at[h], q_out.at[:, :, cols(h)], out_sem.at[1, h]),
        )

    def scale(h, c):
        res = (lin[h] * inv_ref[...] * gain_ref[cols(h)][None, :]).astype(BF16).reshape(2, TOK, DH)
        lin_res[h] = res
        q_res[h] = ((sq_in[:, :, cols(h)].astype(F32) + res.astype(F32)) * SCALE).astype(BF16)
        for x in result_copies(h):
            x.start()
        return c

    lax.fori_loop(0, HEADS, scale, 0, unroll=2)

    for dz in range(NZ):
        kv_wait(block(-1, dz), 1)
        kv_wait(block(1, dz), 0)
        kv_wait(block(2, dz), 0)
        kv_wait(block(2, dz), 1)
    for h in range(HEADS):
        for x in result_copies(h):
            x.wait()
    for c in own:
        c.wait()
    for c in sends:
        c.wait_send()
    for i in range(1, NZ):
        u_copy(i).wait_send()
    for i in range(1, NY):

        @pl.when(y + i < NY)
        def _(i=i):
            total_copy(i, y).wait_send()


def linear_part(*operands):
    hbm = pl.BlockSpec(memory_space=pl.ANY)
    dma = pltpu.SemaphoreType.DMA
    V = pltpu.VMEM
    mat = (DH, DH)
    return pl.pallas_call(
        linear_kernel,
        out_shape=(
            jax.ShapeDtypeStruct((2, TOK, HEADS * DH), BF16),
            jax.ShapeDtypeStruct((2, TOK, HEADS * DH), BF16),
            jax.ShapeDtypeStruct((NSEQ * TOK, DH), BF16),
            jax.ShapeDtypeStruct((NSEQ * TOK, DH), BF16),
        ),
        in_specs=[hbm] * 8,
        out_specs=(hbm,) * 4,
        scratch_shapes=[
            V((2, TOK, HEADS * DH), BF16),
            V((TOK, HEADS * DH), BF16),
            V((TOK, HEADS * DH), BF16),
            V((HEADS, TOK), F32),
            V((HEADS * DH,), F32),
            V((2, TOK, HEADS * DH), BF16),
            V((HEADS, 2, TOK, DH), BF16),
            V((HEADS, 2, TOK, DH), BF16),
            V(mat, F32),
            V((HEADS, DH), F32),
            V((HEADS,) + mat, F32),
            V((2 * TOK, DH), F32),
            V((NZ,) + mat, BF16),
            V((NZ,) + mat, BF16),
            V((8, DH), F32),
            V((NZ, 8, DH), F32),
            V((8, DH), F32),
            V((NY, 8, DH), F32),
            V(mat, BF16),
            V((NY,) + mat, BF16),
            V((NZ,) + mat, BF16),
            V((HEADS,) + mat, BF16),
            V((HEADS, 2 * TOK, DH), F32),
            V((8, 2 * TOK), F32),
            V((NX, 8, 2 * TOK), F32),
            dma((6,)),
            dma((2, HEADS)),
            dma((2,)),
            dma((62,)),
            dma((NSEQ, 2)),
            dma((NZ,)), dma((NZ,)),
            dma((NZ,)), dma((NZ,)),
            dma((NY,)), dma((NY,)),
            dma((NY,)), dma((NY,)),
            dma((NZ,)), dma((NZ,)),
            dma((NX,)), dma((NX,)),
        ],
        compiler_params=pltpu.CompilerParams(
            collective_id=0, has_side_effects=True, vmem_limit_bytes=56 * 2**20
        ),
        cost_estimate=pl.CostEstimate(flops=240_000_000, bytes_accessed=5_000_000, transcendentals=300_000),
        name="linear_and_gather",
    )(*operands)


def softmax_kernel(
    mask_hbm, lin_hbm, q_hbm, k_all, v_all,
    lin_out, soft_out,
    mask, lin_ref, res, order, kaug, vaug, qaug, m_ref, acc, in_sem, out_sem, q_sem, k_sem, v_sem,
):
    me = lax.axis_index("seq")

    def rows(i, size=TOK):
        return pl.ds(pl.multiple_of(i * size, size), size)

    def copies(i):
        r = rows(i, STEP)
        return (
            pltpu.make_async_copy(k_all.at[r], kaug.at[r, pl.ds(0, DH)], k_sem.at[i]),
            pltpu.make_async_copy(v_all.at[r], vaug.at[r, pl.ds(0, DH)], v_sem.at[i]),
        )

    fetch_mask = pltpu.make_async_copy(mask_hbm, mask, in_sem.at[0])
    fetch_mask.start()
    parts = me // STEP_BLOCKS + 1

    def load(i, c):
        for x in copies(i):
            x.start()
        return c

    lax.fori_loop(0, parts, load, 0)
    fetch_q = [
        pltpu.make_async_copy(
            q_hbm.at[j, :, pl.ds(h * DH, DH)], qaug.at[h, pl.ds(j * TOK, TOK), pl.ds(0, DH)], q_sem.at[h, j]
        )
        for h in range(HEADS)
        for j in range(2)
    ]
    for c in fetch_q:
        c.start()
    fetch_lin = pltpu.make_async_copy(lin_hbm, lin_ref, in_sem.at[1])
    fetch_lin.start()

    row = lax.broadcasted_iota(jnp.int32, (TOK, TOK), 0)
    col = lax.broadcasted_iota(jnp.int32, (TOK, TOK), 1)
    pick = (row == col).astype(BF16)
    for h in range(HEADS):
        for j in range(2):
            qaug[h, j * TOK : (j + 1) * TOK, DH:] = pick
    kaug[:, DH:] = jnp.zeros(((NSEQ + 1) * TOK, DH), BF16)
    vaug[:, DH:] = jnp.ones(((NSEQ + 1) * TOK, DH), BF16)
    kaug[NSEQ * TOK :, :DH] = jnp.zeros((TOK, DH), BF16)
    vaug[NSEQ * TOK :, :DH] = jnp.zeros((TOK, DH), BF16)
    kaug[NSEQ * TOK :, DH:] = jnp.full((TOK, DH), NEG, F32).astype(BF16)
    kaug[rows(me), DH:] = jnp.where(row <= col, 0.0, NEG).astype(BF16)
    m_ref[...] = jnp.full_like(m_ref, -3e38)
    acc[...] = jnp.zeros_like(acc)

    fetch_mask.wait()
    order[0] = me
    count = jnp.int32(1)
    for b in range(NSEQ - 1):
        order[count] = b
        count = count + jnp.where(b < me, mask[me, b], 0)
    steps = (count + STEP_BLOCKS - 1) // STEP_BLOCKS
    for n in range(STEP_BLOCKS - 1):
        order[count + n] = NSEQ

    for c in fetch_q:
        c.wait()
    fetch_lin.wait()
    keep_lin = pltpu.make_async_copy(lin_ref, lin_out, out_sem.at[HEADS])
    keep_lin.start()

    def arrive(i, c):
        for x in copies(i):
            x.wait()
        return c

    lax.fori_loop(0, parts, arrive, 0)

    def step(i, c):
        places = [rows(order[i * STEP_BLOCKS + n]) for n in range(STEP_BLOCKS)]

        def head(h, c):
            s = dot_t(qaug[h], jnp.concatenate([kaug[r, :] for r in places], axis=0))
            old = m_ref[h]
            top = jnp.maximum(old, jnp.max(s, axis=1, keepdims=True))
            m_ref[h] = top
            keep = jnp.exp2(old - top)
            p = jnp.concatenate(
                [jnp.exp2(s[:, n * DH : (n + 1) * DH] - top).astype(BF16) for n in range(STEP_BLOCKS)], axis=1
            )
            new = dot(p, jnp.concatenate([vaug[r, :] for r in places], axis=0))
            acc[h, :, :DH] = acc[h, :, :DH] * keep + new[:, :DH]
            acc[h, :, DH:] = acc[h, :, DH:] * keep + new[:, DH:]
            return c

        return lax.fori_loop(0, HEADS, head, c, unroll=HEAD_UNROLL)

    lax.fori_loop(0, steps, step, 0)

    def out_copy(h):
        return pltpu.make_async_copy(res.at[h], soft_out.at[:, :, cols(h)], out_sem.at[h])

    def finish(h, c):
        res[h] = (acc[h, :, :DH] / acc[h, :, DH:]).astype(BF16).reshape(2, TOK, DH)
        out_copy(h).start()
        return c

    lax.fori_loop(0, HEADS, finish, 0, unroll=2)
    keep_lin.wait()
    for h in range(HEADS):
        out_copy(h).wait()


def softmax_part(*operands):
    hbm = pl.BlockSpec(memory_space=pl.ANY)
    V = pltpu.VMEM
    out = jax.ShapeDtypeStruct((2, TOK, HEADS * DH), BF16)
    return pl.pallas_call(
        softmax_kernel,
        out_shape=(out, out),
        in_specs=[hbm] * 5,
        out_specs=(hbm, hbm),
        scratch_shapes=[
            pltpu.SMEM((NSEQ, NSEQ), jnp.int32),
            V((2, TOK, HEADS * DH), BF16),
            V((HEADS, 2, TOK, DH), BF16),
            pltpu.SMEM((NSEQ + STEP_BLOCKS,), jnp.int32),
            V(((NSEQ + 1) * TOK, 2 * DH), BF16),
            V(((NSEQ + 1) * TOK, 2 * DH), BF16),
            V((HEADS, 2 * TOK, 2 * DH), BF16),
            V((HEADS, 2 * TOK, DH), F32),
            V((HEADS, 2 * TOK, 2 * DH), F32),
            pltpu.SemaphoreType.DMA((2,)),
            pltpu.SemaphoreType.DMA((HEADS + 1,)),
            pltpu.SemaphoreType.DMA((HEADS, 2)),
            pltpu.SemaphoreType.DMA((NSEQ // STEP_BLOCKS,)),
            pltpu.SemaphoreType.DMA((NSEQ // STEP_BLOCKS,)),
        ],
        compiler_params=pltpu.CompilerParams(vmem_limit_bytes=56 * 2**20),
        cost_estimate=pl.CostEstimate(flops=6_000_000_000, bytes_accessed=5_000_000, transcendentals=6_000_000),
        name="softmax_attention",
    )(*operands)


def local(lin_queries, lin_keys, lin_values, log_decay, norm_gain, soft_queries, soft_keys, soft_values, block_mask):
    lin, q, k_all, v_all = linear_part(
        lin_queries, lin_keys, lin_values, log_decay.T, norm_gain, soft_keys, soft_values, soft_queries
    )
    return softmax_part(block_mask, lin, q, k_all, v_all)


def solution(mesh):
    return jax.shard_map(
        local,
        mesh=mesh,
        in_specs=(
            P(None, "seq", "head"),
            P("seq", "head"),
            P("seq", "head"),
            P("seq", "head"),
            P("head"),
            P(None, "seq", "head"),
            P("seq", "head"),
            P("seq", "head"),
            P(),
        ),
        out_specs=(P(None, "seq", "head"), P(None, "seq", "head")),
        check_vma=False,
    )
```
